32 devices in a mesh: section: 2 (over core), dp: 16 (over z, y, x).
Axes of the slice: x: 2, y: 2, z: 4, core: 2. Of those that a mesh axis runs over, the one named last changes fastest.
Arguments:
- ends: bfloat16 [2, 48, 282, 768], P('section', 'dp'), may hold values from -6 to 6
- counts: int32 [48], P('dp'), may hold values from 194 to 282, as said below
- keep: int32 [2, 48, 2], P('section', 'dp'), may hold values 0 or 1
- attn_gain: float32 [2, 768], P('section'), may hold values from 0.1 to 1.9
- attn_shift: float32 [2, 768], P('section'), may hold values from -4 to 4
- qkv_weight: bfloat16 [2, 768, 2304], P('section'), may hold values from -0.21875 to 0.21875
- query_bias: float32 [2, 768], P('section'), may hold values from -6 to 6
- value_bias: float32 [2, 768], P('section'), may hold values from -6 to 6
- proj_weight: bfloat16 [2, 768, 768], P('section'), may hold values from -1.25 to 1.25
- proj_bias: float32 [2, 768], P('section'), may hold values from -4 to 4
- mlp_gain: float32 [2, 768], P('section'), may hold values from 0.1 to 1.9
- mlp_shift: float32 [2, 768], P('section'), may hold values from -4 to 4
- up_weight: bfloat16 [2, 768, 3072], P('section'), may hold values from -0.21875 to 0.21875
- up_bias: float32 [2, 3072], P('section'), may hold values from -6 to 6
- down_weight: bfloat16 [2, 3072, 768], P('section'), may hold values from -0.109375 to 0.109375
- down_bias: float32 [2, 768], P('section'), may hold values from -4 to 4
Outputs:
- ends_out: bfloat16 [2, 48, 282, 768], P('section', 'dp')
- grad_attn_gain: float32 [2, 768], P('section')
- grad_attn_shift: float32 [2, 768], P('section')
- grad_qkv_weight: float32 [2, 768, 2304], P('section')
- grad_query_bias: float32 [2, 768], P('section')
- grad_value_bias: float32 [2, 768], P('section')
- grad_proj_weight: float32 [2, 768, 768], P('section')
- grad_proj_bias: float32 [2, 768], P('section')
- grad_mlp_gain: float32 [2, 768], P('section')
- grad_mlp_shift: float32 [2, 768], P('section')
- grad_up_weight: float32 [2, 768, 3072], P('section')
- grad_up_bias: float32 [2, 3072], P('section')
- grad_down_weight: float32 [2, 3072, 768], P('section')
- grad_down_bias: float32 [2, 768], P('section')
- rms: float32 [2, 3], P('section')
The draws below stay inside these ranges and needn't reach their ends.
Inputs may be any that keep to these rules, and one draw needn't show every extreme that they name: Valid slots of each image; its first counts slots are tokens, the rest padding. Some image has 282 and some has 194.
All inputs are finite; a program needn't handle non-finite values. No bound on the sum of `keep` on one device may be relied on, other than what follows from the above.
Results may differ from the reference program's by a relative error of at most 0.012.
Values may be sent and summed in bfloat16 or wider, within the bound.
No kernel may reach another device: no remote copies, remote signals or barrier semaphores. Data moves between devices by JAX's collectives and lax.ppermute only.
A program may use at most 320 MiB of HBM per device.

```python
import jax
import jax.numpy as jnp
from jax import lax

D = 768
HEADS = 12
HEAD = 64
FF = 3072
SLOTS = 282
MIN_VALID = 194
IMG_DEV = 3
IMAGES = 48
N_DP = 16


def draw_counts(key, part):
    key = jax.random.fold_in(key, 11)
    first_key, second_key, third_key = jax.random.split(key, 3)
    values = jax.random.randint(first_key, (IMAGES,), MIN_VALID, SLOTS + 1)
    highest = jax.random.randint(second_key, (), 0, IMAGES)
    offset = jax.random.randint(third_key, (), 1, IMAGES)
    lowest = (highest + offset) % IMAGES
    position = jnp.arange(IMAGES)
    values = jnp.where(position == highest, SLOTS, values)
    values = jnp.where(position == lowest, MIN_VALID, values)
    return values.astype(jnp.int32)


def plant(entries, stream_key, low, top_value):
    extent = entries.shape
    index_at = [jax.random.randint(jax.random.fold_in(stream_key, axis), (), 0, extent[axis]) for axis in range(len(extent))]
    entries = entries.at[tuple(index_at)].set(low)
    longest = extent.index(max(extent))
    index_at[longest] = (index_at[longest] + 1) % extent[longest]
    return entries.at[tuple(index_at)].set(top_value)


def steps_of(own_key, dims, cuts, smallest, largest):
    def one(axis_at, parts):
        steps = jax.random.uniform(jax.random.fold_in(jax.random.fold_in(own_key, 6), axis_at), (parts,), jnp.float32, smallest / len(cuts), largest / len(cuts))
        return jnp.repeat(jnp.exp(steps), dims[axis_at] // parts).reshape((-1,) + (1,) * (len(dims) - axis_at - 1))

    level = one(*cuts[0])
    for cut in cuts[1:]:
        level = level * one(*cut)
    return level


def gaussian(rng, shape, width, most, shards=(), held_as=jnp.bfloat16):
    factor_of = steps_of(rng, shape, shards, -0.22, 0.18) if shards else 1.0
    entries = jax.random.normal(rng, shape, jnp.float32) * width * factor_of
    return jnp.minimum(jnp.maximum(entries, -most), most).astype(held_as)


def setup_inputs(seed: int = 0) -> dict:
    key_list = jax.random.split(jax.random.key(seed), 17)
    ends = gaussian(key_list[0], (2, IMAGES, SLOTS, D), 1.0, 6.0, ((0, 2), (1, 16)))
    counts = draw_counts(jax.random.fold_in(key_list[16], 71), 0)
    keep = plant((jax.random.randint(key_list[2], (2, IMAGES, 2), 0, 4) < 3).astype(jnp.int32), jax.random.fold_in(key_list[2], 1), 0, 1)
    attn_gain = jnp.clip(1.0 + 0.18 * jax.random.normal(key_list[3], (2, D), jnp.float32), 0.1, 1.9)
    attn_shift = gaussian(key_list[4], (2, D), 0.3, 4.0, ((0, 2),), jnp.float32)
    qkv_weight = gaussian(key_list[5], (2, D, 3 * D), D ** -0.5, 0.21875, ((0, 2),))
    query_bias = gaussian(key_list[6], (2, D), 0.5, 6.0, ((0, 2),), jnp.float32)
    value_bias = gaussian(key_list[7], (2, D), 0.5, 6.0, ((0, 2),), jnp.float32)
    proj_weight = gaussian(key_list[8], (2, D, D), (D // 32) ** -0.5, 1.25, ((0, 2),))
    proj_bias = gaussian(key_list[9], (2, D), 0.3, 4.0, ((0, 2),), jnp.float32)
    mlp_gain = jnp.clip(1.0 + 0.18 * jax.random.normal(key_list[10], (2, D), jnp.float32), 0.1, 1.9)
    mlp_shift = gaussian(key_list[11], (2, D), 0.3, 4.0, ((0, 2),), jnp.float32)
    up_weight = gaussian(key_list[12], (2, D, FF), D ** -0.5, 0.21875, ((0, 2),))
    up_bias = gaussian(key_list[13], (2, FF), 0.5, 6.0, ((0, 2),), jnp.float32)
    down_weight = gaussian(key_list[14], (2, FF, D), FF ** -0.5, 0.109375, ((0, 2),))
    down_bias = gaussian(key_list[15], (2, D), 0.3, 4.0, ((0, 2),), jnp.float32)
    return {"ends": ends, "counts": counts, "keep": keep, "attn_gain": attn_gain, "attn_shift": attn_shift, "qkv_weight": qkv_weight, "query_bias": query_bias, "value_bias": value_bias, "proj_weight": proj_weight, "proj_bias": proj_bias, "mlp_gain": mlp_gain, "mlp_shift": mlp_shift, "up_weight": up_weight, "up_bias": up_bias, "down_weight": down_weight, "down_bias": down_bias}


keep_scale = 4.0 / 3.0
eps_norm = 1e-06

@jax.custom_vjp
def low(v):
    return lax.optimization_barrier(v.astype(jnp.bfloat16)).astype(jnp.float32)

@jax.custom_vjp
def low_back(v):
    return v

def low_keep(v):
    return (low(v), None)

def low_pass(kept, grad):
    return (grad,)

def back_keep(v):
    return (v, None)

def back_low(kept, grad):
    return (low(grad),)
low.defvjp(low_keep, low_pass)
low_back.defvjp(back_keep, back_low)

def product(form, left, right):
    return jnp.einsum(form, left, right, precision=lax.Precision.HIGHEST)

def layer_norm(stream, gain, shift):
    centred = stream - lax.optimization_barrier(jnp.mean(stream, axis=-1, keepdims=True))
    normed = centred * lax.rsqrt(lax.optimization_barrier(jnp.mean(centred * centred, axis=-1, keepdims=True)) + eps_norm)
    return normed * gain + shift

def block_layer(stream, weights, valid, keeping):
    attn_gain, attn_shift, qkv_weight, query_bias, value_bias, proj_weight, proj_bias, mlp_gain, mlp_shift, up_weight, up_bias, down_weight, down_bias = weights
    images = stream.shape[0]
    split_shape = (images, SLOTS, HEADS, HEAD)
    normed_in = low(layer_norm(stream, attn_gain, attn_shift))
    joined = product('bsd,de->bse', normed_in, qkv_weight)
    queries = low_back(low(joined[..., :D] + query_bias))
    key_rows = low_back(low(joined[..., D:2 * D]))
    value_rows = low_back(low(joined[..., 2 * D:] + value_bias))
    scores = product('bqhe,bkhe->bhqk', queries.reshape(split_shape), key_rows.reshape(split_shape)) * HEAD ** (-0.5)
    scores = low_back(scores)
    live = jnp.arange(SLOTS)[None, None, None, :] < valid[:, None, None, None]
    scores = jnp.where(live, scores, -1e+30)
    attention = jax.nn.softmax(scores, axis=-1)
    mixed = product('bhqk,bkhe->bqhe', low(attention), value_rows.reshape(split_shape)).reshape(images, SLOTS, D)
    mixed = low_back(low(mixed))
    attn_branch = keeping[:, 0, None, None] * low_back(product('bsd,de->bse', mixed, proj_weight) + proj_bias)
    middle = stream + attn_branch
    mlp_in = low(layer_norm(middle, mlp_gain, mlp_shift))
    hidden = low_back(product('bsd,df->bsf', mlp_in, up_weight) + up_bias)
    active = low(jax.nn.gelu(hidden, approximate=False))
    mlp_branch = keeping[:, 1, None, None] * low_back(product('bsf,fd->bsd', active, down_weight) + down_bias)
    return (middle + mlp_branch, attn_branch, mlp_branch)

def reference(ends, counts, keep, attn_gain, attn_shift, qkv_weight, query_bias, value_bias, proj_weight, proj_bias, mlp_gain, mlp_shift, up_weight, up_bias, down_weight, down_bias):
    params = tuple((item.astype(jnp.float32) for item in (attn_gain, attn_shift, qkv_weight, query_bias, value_bias, proj_weight, proj_bias, mlp_gain, mlp_shift, up_weight, up_bias, down_weight, down_bias)))
    first_input = ends[0].astype(jnp.float32)
    cotangent = ends[1].astype(jnp.float32)
    keep_all = keep.astype(jnp.float32) * keep_scale

    def run(weights, inputs):

        def one_group(operands):
            stream, valid, keeping = operands
            rows = (jnp.arange(SLOTS)[None, :] < valid[:, None]).astype(jnp.float32)[..., None]
            first_layer = tuple((item[0] for item in weights))
            second_layer = tuple((item[1] for item in weights))
            out_one, attn_one, mlp_one = block_layer(stream, first_layer, valid, keeping[0])
            sent = low_back(low(out_one))
            out_two, attn_two, mlp_two = block_layer(sent, second_layer, valid, keeping[1])
            sums = jnp.stack([jnp.stack([jnp.sum(out_one * out_one * rows), jnp.sum(attn_one * attn_one * rows), jnp.sum(mlp_one * mlp_one * rows)]), jnp.stack([jnp.sum(out_two * out_two * rows), jnp.sum(attn_two * attn_two * rows), jnp.sum(mlp_two * mlp_two * rows)])])
            return (out_two * rows, sums)
        grouped = inputs.reshape(N_DP, IMG_DEV, SLOTS, D)
        valid_groups = counts.reshape(N_DP, IMG_DEV)
        keep_groups = jnp.transpose(keep_all.reshape(2, N_DP, IMG_DEV, 2), (1, 0, 2, 3))
        outputs, sums = lax.map(jax.checkpoint(one_group), (grouped, valid_groups, keep_groups))
        return (outputs.reshape(IMAGES, SLOTS, D), lax.optimization_barrier(jnp.sum(sums, axis=0)))
    result, pullback, sums = jax.vjp(run, params, first_input, has_aux=True)
    grads, grad_input = pullback(cotangent)
    total = jnp.sum(counts.astype(jnp.float32))
    rms = jnp.sqrt(sums / (total * D))
    ends_out = jnp.stack([grad_input.astype(jnp.bfloat16), result.astype(jnp.bfloat16)])
    return (ends_out, grads[0], grads[1], grads[2], grads[3], grads[4], grads[5], grads[6], grads[7], grads[8], grads[9], grads[10], grads[11], grads[12], rms)
```

```python
import functools

import jax
import jax.numpy as jnp
from jax import lax
from jax.experimental import pallas as pl
from jax.experimental.pallas import tpu as pltpu
from jax.sharding import PartitionSpec as P

HEADS = 12
CHUNKS = 16
TILE = 256
KEEP_SCALE = 4.0 / 3.0
EPS = 1e-06
F32 = jnp.float32
BF16 = jnp.bfloat16
VMEM = pl.BlockSpec(memory_space=pltpu.VMEM)
SMEM = pl.BlockSpec(memory_space=pltpu.SMEM)


def dot_nn(left, right):
    return lax.dot_general(left, right, (((1,), (0,)), ((), ())), preferred_element_type=F32)


def dot_nt(left, right):
    return lax.dot_general(left, right, (((1,), (1,)), ((), ())), preferred_element_type=F32)


def dot_tn(left, right):
    return lax.dot_general(left, right, (((0,), (0,)), ((), ())), preferred_element_type=F32)


def call(body, operands, outs, scratch=(), flops=0, limit=48):
    in_specs = [SMEM if jnp.issubdtype(o.dtype, jnp.integer) or o.ndim == 1 else VMEM for o in operands]
    out_specs = [SMEM if o.shape == (8,) else VMEM for o in outs]
    moved = sum(o.size * o.dtype.itemsize for o in operands) + sum(
        o.size * o.dtype.itemsize for o in outs
    )
    return pl.pallas_call(
        body,
        out_shape=list(outs),
        in_specs=in_specs,
        out_specs=out_specs,
        scratch_shapes=list(scratch),
        compiler_params=pltpu.CompilerParams(vmem_limit_bytes=limit << 20),
        cost_estimate=pl.CostEstimate(flops=int(flops), bytes_accessed=int(moved), transcendentals=0),
    )(*operands)


def shaped(*shape, dtype=BF16):
    return jax.ShapeDtypeStruct(shape, dtype)


def standardize(stream):
    centred = stream - jnp.mean(stream, axis=-1, keepdims=True)
    inverse = lax.rsqrt(jnp.mean(centred * centred, axis=-1, keepdims=True) + EPS)
    return centred * inverse, inverse


def norm_back(grad, normed, inverse):
    return inverse * (
        grad
        - jnp.mean(grad, axis=-1, keepdims=True)
        - normed * jnp.mean(grad * normed, axis=-1, keepdims=True)
    )


def lanes(start, size):
    return pl.ds(pl.multiple_of(start, 128), size)


def rows_at(start, size):
    return pl.ds(pl.multiple_of(start, 16), size)


def row_mask(length, valid):
    return lax.broadcasted_iota(jnp.int32, (length, 1), 0) < valid


def qkv_kernel(length, images, act, x, gain, shift, weight, qb, vb, n1, qkv):
    @pl.when(act[0] == 1)
    def _():
        width = x.shape[1]

        def norm(i, _):
            r = rows_at(i * (length // 2), length // 2)
            normed, _inv = standardize(x[r, :].astype(F32))
            n1[r, :] = (normed * gain[...] + shift[...]).astype(BF16)
            return 0

        lax.fori_loop(0, images * 2, norm, 0)
        tiles = width // TILE
        for part, bias in ((0, qb), (1, None), (2, vb)):

            def tile(t, _, part=part, bias=bias):
                at = lanes(part * width + t * TILE, TILE)
                out = dot_nn(n1[...], weight[:, at])
                if bias is not None:
                    out = out + bias[:, lanes(t * TILE, TILE)]
                qkv[:, at] = out.astype(BF16)
                return 0

            lax.fori_loop(0, tiles, tile, 0)


def attend_kernel(length, images, act, valid, qkv, probs, mixed):
    width = mixed.shape[1]
    pairs = width // 128
    low = lax.broadcasted_iota(jnp.int32, (1, 128), 1) < 64

    @pl.when(act[0] == 1)
    def _():
        def pair(step, _):
            i = step // pairs
            p = step - i * pairs
            r = rows_at(i * length, length)
            q = qkv[r, lanes(p * 128, 128)] * jnp.asarray(0.125, BF16)
            k = qkv[r, lanes(width + p * 128, 128)]
            v = qkv[r, lanes(2 * width + p * 128, 128)]
            zero = jnp.zeros_like(q)
            stacked = jnp.concatenate([jnp.where(low, q, zero), jnp.where(low, zero, q)], axis=0)
            scores = dot_nt(stacked, k)
            live = lax.broadcasted_iota(jnp.int32, (1, length), 1) < valid[i]
            scores = jnp.where(live, scores, -1e30)
            top = jnp.max(scores, axis=-1, keepdims=True)
            e = jnp.exp(scores - top)
            total = jnp.sum(e, axis=-1, keepdims=True)
            prob = (e * (1.0 / total)).astype(BF16)
            probs[rows_at(step * 2 * length, 2 * length), :] = prob
            out = dot_nn(prob, v)
            mixed[r, lanes(p * 128, 128)] = jnp.where(low, out[:length], out[length:]).astype(BF16)
            return 0

        lax.fori_loop(0, images * pairs, pair, 0)


def up_kernel(
    length, images, act, keep, valid, x, mixed, pw, pb, gain, shift, uw, ub, h1, n2, slope, gact, stat
):
    @pl.when(act[0] == 1)
    def _():
        width = x.shape[1]
        hidden = gact.shape[1]
        total = jnp.zeros((length, width), F32)
        for i in range(images):
            r = slice(i * length, (i + 1) * length)
            a = keep[2 * i] * (dot_nn(mixed[r, :], pw[...]) + pb[...])
            total = total + jnp.where(row_mask(length, valid[i]), a * a, 0.0)
            h = x[r, :].astype(F32) + a
            h1[r, :] = h
            normed, _inv = standardize(h)
            n2[r, :] = (normed * gain[...] + shift[...]).astype(BF16)
        stat[0] = jnp.sum(total)

        def tile(t, _):
            at = lanes(t * TILE, TILE)
            for i in range(images):
                r = slice(i * length, (i + 1) * length)
                u = dot_nn(n2[r, :], uw[:, at]) + ub[:, at]
                cdf = 0.5 * (1.0 + lax.erf(u * 0.7071067811865476))
                gact[r, at] = (u * cdf).astype(BF16)
                slope[r, at] = (cdf + u * (jnp.exp(-0.5 * u * u) * 0.3989422804014327)).astype(BF16)
            return 0

        lax.fori_loop(0, hidden // TILE, tile, 0)


def down_kernel(length, images, act, keep, valid, h1, gact, dw, db, h2, stat):
    @pl.when(act[0] == 1)
    def _():
        width = h1.shape[1]
        tiles = width // TILE
        stat[0] = 0.0
        stat[1] = 0.0

        def tile(step, _):
            i = step // tiles
            r = rows_at(i * length, length)
            at = lanes((step - i * tiles) * TILE, TILE)
            m = keep[2 * i + 1] * (dot_nn(gact[r, :], dw[:, at]) + db[:, at])
            h = h1[r, at] + m
            mask = row_mask(length, valid[i])
            stat[0] += jnp.sum(jnp.where(mask, h * h, 0.0))
            stat[1] += jnp.sum(jnp.where(mask, m * m, 0.0))
            h2[r, at] = h.astype(BF16)
            return 0

        lax.fori_loop(0, images * tiles, tile, 0)


def scatter_chunks(code, unit, chunk_of, pieces):
    starts = (8, 4, 2, 1, 0)
    counts = (8, 4, 2, 1, 1)
    for ref, start, count in zip(pieces, starts, counts):
        for j in range(count):
            which = jnp.bitwise_xor(code, start + j)
            chunk_of(which, ref, j * unit)


def down_back_kernel(length, images, act, code, keep, dh2, gact, slope, dw, *refs):
    *pieces, du, vec, dz, full = refs

    @pl.when(act[0] == 1)
    def _():
        width = dh2.shape[1]
        hidden = gact.shape[1]
        total = jnp.zeros((1, width), F32)
        for i in range(images):
            r = slice(i * length, (i + 1) * length)
            z = (keep[2 * i + 1] * dh2[r, :].astype(F32)).astype(BF16)
            dz[r, :] = z
            total = total + jnp.sum(z.astype(F32), axis=0, keepdims=True)
        vec[0:1, :] = total

        def wtile(t, _):
            at = pl.multiple_of(t * 512, 512)
            full[pl.ds(at, 512), :] = dot_tn(gact[:, pl.ds(at, 512)], dz[...]).astype(BF16)
            return 0

        lax.fori_loop(0, hidden // 512, wtile, 0)
        unit = hidden // CHUNKS

        def move(which, ref, at):
            ref[at : at + unit, :] = full[rows_at(which * unit, unit), :]

        scatter_chunks(code[0], unit, move, pieces)

        def tile(t, _):
            at = lanes(t * TILE, TILE)
            d = dot_nt(dz[...], dw[rows_at(t * TILE, TILE), :])
            d = (d * slope[:, at].astype(F32)).astype(BF16)
            du[:, at] = d
            return 0

        lax.fori_loop(0, hidden // TILE, tile, 0)


def up_back_kernel(
    length, images, act, code, keep, dh2, n2, du, uw, h1, gain, mixed, pw, *refs
):
    *pieces, dh1, dmix, vec, uvec, dy, upf, projf = refs

    @pl.when(act[0] == 1)
    def _():
        width = dh2.shape[1]
        hidden = du.shape[1]

        def wtile(t, _):
            at = lanes(t * 512, 512)
            upf[:, at] = dot_tn(n2[...], du[:, at]).astype(BF16)
            uvec[:, at] = jnp.sum(du[:, at].astype(F32), axis=0, keepdims=True)
            return 0

        lax.fori_loop(0, hidden // 512, wtile, 0)
        dgain = jnp.zeros((1, width), F32)
        dshift = jnp.zeros((1, width), F32)
        dpb = jnp.zeros((1, width), F32)
        for i in range(images):
            r = slice(i * length, (i + 1) * length)
            dn2 = dot_nt(du[r, :], uw[...])
            normed, inverse = standardize(h1[r, :])
            dgain = dgain + jnp.sum(dn2 * normed, axis=0, keepdims=True)
            dshift = dshift + jnp.sum(dn2, axis=0, keepdims=True)
            d = dh2[r, :].astype(F32) + norm_back(dn2 * gain[...], normed, inverse)
            dh1[r, :] = d
            y = (keep[2 * i] * d).astype(BF16)
            dy[r, :] = y
            dpb = dpb + jnp.sum(y.astype(F32), axis=0, keepdims=True)
            dmix[r, :] = dot_nt(y, pw[...]).astype(BF16)
        vec[0:1, :] = dgain
        vec[1:2, :] = dshift
        vec[2:3, :] = dpb
        projf[...] = dot_tn(mixed[...], dy[...]).astype(BF16)
        blocks = hidden // width
        unit = width // CHUNKS
        whole = unit * (blocks + 1)

        def move(which, ref, at):
            r = rows_at(which * unit, unit)
            for b in range(blocks):
                ref[at + b * unit : at + (b + 1) * unit, :] = upf[r, b * width : (b + 1) * width]
            ref[at + blocks * unit : at + whole, :] = projf[r, :]

        scatter_chunks(code[0], whole, move, pieces)


def attend_back_kernel(length, images, act, qkv, probs, mixed, dmix, dj):
    width = mixed.shape[1]
    pairs = width // 128
    low = lax.broadcasted_iota(jnp.int32, (1, 128), 1) < 64

    @pl.when(act[0] == 1)
    def _():
        def pair(step, _):
            i = step // pairs
            p = step - i * pairs
            r = rows_at(i * length, length)
            at = lanes(p * 128, 128)
            k_at = lanes(width + p * 128, 128)
            v_at = lanes(2 * width + p * 128, 128)
            scale = jnp.asarray(0.125, BF16)
            q = qkv[r, at] * scale
            k = qkv[r, k_at]
            v = qkv[r, v_at]
            o = mixed[r, at].astype(F32)
            g = dmix[r, at]

            def stack(a):
                zero = jnp.zeros_like(a)
                return jnp.concatenate([jnp.where(low, a, zero), jnp.where(low, zero, a)], axis=0)

            both = stack(g)
            prod = g.astype(F32) * o
            side = jnp.concatenate(
                [
                    jnp.sum(jnp.where(low, prod, 0.0), axis=-1, keepdims=True),
                    jnp.sum(jnp.where(low, 0.0, prod), axis=-1, keepdims=True),
                ],
                axis=0,
            )
            prob = probs[rows_at(step * 2 * length, 2 * length), :]
            dp = dot_nt(both, v)
            ds = (prob.astype(F32) * (dp - side)).astype(BF16)
            dj[r, v_at] = dot_tn(prob, both).astype(BF16)
            dq = dot_nn(ds, k)
            dj[r, at] = (0.125 * jnp.where(low, dq[:length], dq[length:])).astype(BF16)
            dj[r, k_at] = dot_tn(ds, stack(q)).astype(BF16)
            return 0

        lax.fori_loop(0, images * pairs, pair, 0)


def qkv_back_kernel(length, images, act, code, x, n1, dj, weight, gain, dh1, *refs):
    *pieces, dx, vec, full = refs

    @pl.when(act[0] == 1)
    def _():
        width = x.shape[1]
        three = dj.shape[1]

        def wtile(t, _):
            at = lanes(t * TILE, TILE)
            full[:, at] = dot_tn(n1[...], dj[:, at]).astype(BF16)
            return 0

        lax.fori_loop(0, three // TILE, wtile, 0)
        dgain = jnp.zeros((1, width), F32)
        dshift = jnp.zeros((1, width), F32)
        dqb = jnp.zeros((1, width), F32)
        dvb = jnp.zeros((1, width), F32)
        for i in range(images):
            r = slice(i * length, (i + 1) * length)
            dqb = dqb + jnp.sum(dj[r, 0:width].astype(F32), axis=0, keepdims=True)
            dvb = dvb + jnp.sum(dj[r, 2 * width :].astype(F32), axis=0, keepdims=True)
            dn1 = dot_nt(dj[r, :], weight[...])
            normed, inverse = standardize(x[r, :].astype(F32))
            dgain = dgain + jnp.sum(dn1 * normed, axis=0, keepdims=True)
            dshift = dshift + jnp.sum(dn1, axis=0, keepdims=True)
            d = dh1[r, :] + norm_back(dn1 * gain[...], normed, inverse)
            dx[r, :] = d.astype(BF16)
        vec[0:1, :] = dgain
        vec[1:2, :] = dshift
        vec[2:3, :] = dqb
        vec[3:4, :] = dvb
        blocks = three // width
        unit = width // CHUNKS

        def move(which, ref, at):
            r = rows_at(which * unit, unit)
            for b in range(blocks):
                ref[at + b * unit : at + (b + 1) * unit, :] = full[r, b * width : (b + 1) * width]

        scatter_chunks(code[0], blocks * unit, move, pieces)


def piece_shapes(unit, width):
    return [shaped(n * unit, width) for n in (8, 4, 2, 1, 1)]


def forward(act, valid, keep, x, w, length, images):
    (ag, ac, qkvw, qb, vb, pw, pb, mg, mc, uw, ub, dw, db) = w
    tokens, width = x.shape
    hidden = uw.shape[1]
    half = width * width * tokens * 2
    n1, qkv = call(
        functools.partial(qkv_kernel, length, images),
        (act, x, ag, ac, qkvw, qb, vb),
        (shaped(tokens, width), shaped(tokens, 3 * width)),
        flops=3 * half,
    )
    probs, mixed = call(
        functools.partial(attend_kernel, length, images),
        (act, valid, qkv),
        (shaped(images * HEADS * length, length), shaped(tokens, width)),
        flops=2 * half,
    )
    h1, n2, slope, gact, stat_a = call(
        functools.partial(up_kernel, length, images),
        (act, keep, valid, x, mixed, pw, pb, mg, mc, uw, ub),
        (
            shaped(tokens, width, dtype=F32),
            shaped(tokens, width),
            shaped(tokens, hidden),
            shaped(tokens, hidden),
            shaped(8, dtype=F32),
        ),
        flops=5 * half,
    )
    h2, stat_m = call(
        functools.partial(down_kernel, length, images),
        (act, keep, valid, h1, gact, dw, db),
        (shaped(tokens, width), shaped(8, dtype=F32)),
        flops=4 * half,
    )
    stats = jnp.stack([stat_m[0], stat_a[0], stat_m[1]])
    return h2, stats, (x, n1, qkv, probs, mixed, h1, n2, slope, gact)


def down_back(act, code, keep, seed, saved, w, length, images):
    (ag, ac, qkvw, qb, vb, pw, pb, mg, mc, uw, ub, dw, db) = w
    (x, n1, qkv, probs, mixed, h1, n2, slope, gact) = saved
    tokens, width = x.shape
    hidden = uw.shape[1]
    half = width * width * tokens * 2
    *pieces, du, vec = call(
        functools.partial(down_back_kernel, length, images),
        (act, code, keep, seed, gact, slope, dw),
        (
            *piece_shapes(hidden // CHUNKS, width),
            shaped(tokens, hidden),
            shaped(8, width, dtype=F32),
        ),
        scratch=(pltpu.VMEM((tokens, width), BF16), pltpu.VMEM((hidden, width), BF16)),
        flops=8 * half,
    )
    return pieces, du, vec


def up_back(act, code, keep, seed, du, saved, w, length, images):
    (ag, ac, qkvw, qb, vb, pw, pb, mg, mc, uw, ub, dw, db) = w
    (x, n1, qkv, probs, mixed, h1, n2, slope, gact) = saved
    tokens, width = x.shape
    hidden = uw.shape[1]
    half = width * width * tokens * 2
    *pieces, dh1, dmix, vec, uvec = call(
        functools.partial(up_back_kernel, length, images),
        (act, code, keep, seed, n2, du, uw, h1, mg, mixed, pw),
        (
            *piece_shapes((hidden + width) // CHUNKS, width),
            shaped(tokens, width, dtype=F32),
            shaped(tokens, width),
            shaped(8, width, dtype=F32),
            shaped(1, hidden, dtype=F32),
        ),
        scratch=(
            pltpu.VMEM((tokens, width), BF16),
            pltpu.VMEM((width, hidden), BF16),
            pltpu.VMEM((width, width), BF16),
        ),
        flops=10 * half,
    )
    return pieces, dh1, dmix, vec, uvec


def qkv_back(act, code, dh1, dmix, saved, w, length, images):
    (ag, ac, qkvw, qb, vb, pw, pb, mg, mc, uw, ub, dw, db) = w
    (x, n1, qkv, probs, mixed, h1, n2, slope, gact) = saved
    tokens, width = x.shape
    half = width * width * tokens * 2
    (dj,) = call(
        functools.partial(attend_back_kernel, length, images),
        (act, qkv, probs, mixed, dmix),
        (shaped(tokens, 3 * width),),
        flops=4 * half,
    )
    *pieces, dx, vec = call(
        functools.partial(qkv_back_kernel, length, images),
        (act, code, x, n1, dj, qkvw, ag, dh1),
        (
            *piece_shapes(3 * width // CHUNKS, width),
            shaped(tokens, width),
            shaped(8, width, dtype=F32),
        ),
        scratch=(pltpu.VMEM((width, 3 * width), BF16),),
        flops=6 * half,
    )
    return pieces, dx, vec


def orders(bits):
    if bits == 4:
        return ((0, 1, 2, 3), (1, 0, 2, 3), (2, 3, 0, 1))
    plain = tuple(range(bits))
    return (plain, plain, plain)


def flipped(block, bit, sections, size):
    route = [(s * size + i, s * size + (i ^ (1 << bit))) for s in sections for i in range(size)]
    return lax.ppermute(block, ("section", "dp"), route)


def chunk_code(order, place):
    code = jnp.zeros((), jnp.int32)
    for k, bit in enumerate(order):
        code = code + (((place >> bit) & 1) << (len(order) - 1 - k))
    return code


def reduce_parts(pieces, order, sections, size):
    unit = pieces[-1].shape[0]
    if size != CHUNKS:
        whole = lax.psum(jnp.concatenate(pieces[::-1]), "dp")
        return whole[: 8 * unit], whole[8 * unit :]
    arrived = []
    for k in range(4):
        count = unit * (8 >> k)
        part = pieces[k]
        if arrived:
            total = part.astype(F32)
            for r in arrived:
                total = total + r[count : 2 * count].astype(F32)
            part = total.astype(BF16)
        arrived.append(flipped(part, order[k], sections, size))
    total = pieces[4].astype(F32)
    for r in arrived:
        total = total + r[:unit].astype(F32)
    have = total.astype(BF16)
    for k in (3, 2, 1):
        have = jnp.concatenate([have, flipped(have, order[k], sections, size)])
    return have, flipped(have, order[0], sections, size)


def settle(code, use, sets, blocks, shapes):
    unit = sets[0][0].shape[0] // 8
    width = sets[0][0].shape[1]
    rows = unit // sum(blocks)

    def body(scalars, *refs):
        ins, outs = refs[:4], refs[4:]
        j = pl.program_id(0)
        for s in range(2):
            for h in range(2):

                @pl.when((scalars[1] == s) & ((j >= 8) == (h == 1)))
                def _(src=ins[2 * s + h]):
                    at = 0
                    for count, out in zip(blocks, outs):
                        for b in range(count):
                            out[:, b * width : (b + 1) * width] = src[at : at + rows, :].astype(F32)
                            at += rows

    lower = pl.BlockSpec((unit, width), lambda j, s: (jnp.minimum(j, 7), 0))
    upper = pl.BlockSpec((unit, width), lambda j, s: (jnp.maximum(j - 8, 0), 0))
    outs = [shaped(*s, dtype=F32) for s in shapes]
    out_specs = [
        pl.BlockSpec((rows, count * width), lambda j, s: (jnp.bitwise_xor(s[0], j), 0))
        for count in blocks
    ]
    moved = sum(o.size * 4 for o in outs) * 2
    return pl.pallas_call(
        body,
        out_shape=outs,
        grid_spec=pltpu.PrefetchScalarGridSpec(
            num_scalar_prefetch=1,
            grid=(CHUNKS,),
            in_specs=[lower, upper, lower, upper],
            out_specs=out_specs,
        ),
        compiler_params=pltpu.CompilerParams(vmem_limit_bytes=16 << 20),
        cost_estimate=pl.CostEstimate(flops=0, bytes_accessed=moved, transcendentals=0),
    )(jnp.stack([code, use]), *sets[0], *sets[1])


def per_device(size, ends, counts, keep, *params):
    w = [item if item.ndim == 2 else item[0] for item in params]
    section = lax.axis_index("section")
    place = lax.axis_index("dp")
    first = section == 0
    images, slots, width = ends.shape[1:]
    hidden = w[9].shape[1]
    length = -(-slots // 32) * 32
    padded = ((0, 0), (0, length - slots), (0, 0))
    bits = size.bit_length() - 1
    ways = orders(bits)
    if size == CHUNKS:
        codes = [chunk_code(o, place) for o in ways]
    else:
        codes = [jnp.zeros((), jnp.int32)] * 3
    acts = [(section == s).astype(jnp.int32).reshape(1) for s in (0, 1)]
    keeping = (keep[0].astype(F32) * KEEP_SCALE).reshape(-1)
    live = (jnp.arange(slots)[None, :] < counts[:, None])[..., None]

    x0 = jnp.pad(ends[0], padded).reshape(images * length, width)
    seed1 = jnp.pad(jnp.where(live, ends[0], jnp.zeros((), BF16)), padded)
    seed1 = seed1.reshape(images * length, width)

    def crossed(block, source):
        route = [(source * size + i, (1 - source) * size + i) for i in range(size)]
        return lax.ppermute(block, ("section", "dp"), route)

    out0, stats0, saved0 = forward(acts[0], counts, keeping, x0, w, length, images)
    x1 = crossed(out0, 0)
    out1, stats1, saved1 = forward(acts[1], counts, keeping, x1, w, length, images)

    def backward(which, seed, saved):
        act = acts[which]
        scalar = [c.reshape(1) for c in codes]
        pa, du, va = down_back(act, scalar[0], keeping, seed, saved, w, length, images)
        ra = reduce_parts(pa, ways[0], (which,), size)
        pb, dh1, dmix, vb, uvec = up_back(
            act, scalar[1], keeping, seed, du, saved, w, length, images
        )
        rb = reduce_parts(pb, ways[1], (which,), size)
        pc, dx, vc = qkv_back(act, scalar[2], dh1, dmix, saved, w, length, images)
        rc = reduce_parts(pc, ways[2], (which,), size)
        vec = jnp.concatenate([vc[:4], vb[:3], va[:1], uvec.reshape(-1, width)])
        return dx, vec, (ra, rb, rc)

    dx1, vec1, red1 = backward(1, seed1, saved1)
    seed0 = crossed(dx1, 1)
    dx0, vec0, red0 = backward(0, seed0, saved0)

    stats = jnp.where(first, stats0, stats1)
    extra = jnp.concatenate([stats, jnp.sum(counts.astype(F32)).reshape(1)])
    extra = jnp.pad(extra, (0, width - 4)).reshape(1, width)
    vec = jnp.concatenate([jnp.where(first, vec0, vec1), extra])
    for bit in range(bits):
        vec = vec + flipped(vec, bit, (0, 1), size)

    use = section.astype(jnp.int32)
    blocks = hidden // width
    (g_down,) = settle(codes[0], use, (red0[0], red1[0]), (1,), [(hidden, width)])
    g_up, g_proj = settle(
        codes[1], use, (red0[1], red1[1]), (blocks, 1), [(width, hidden), (width, width)]
    )
    (g_qkv,) = settle(codes[2], use, (red0[2], red1[2]), (3,), [(width, 3 * width)])

    shown = jnp.where(first, dx0, out1).reshape(images, length, width)[:, :slots]
    shown = jnp.where(live, shown, jnp.zeros((), BF16))[None]
    rms = jnp.sqrt(vec[-1, 0:3] / (vec[-1, 3] * width)).reshape(1, 3)
    row = lambda k: vec[k : k + 1]
    g_ub = vec[8 : 8 + blocks].reshape(1, hidden)
    return (
        shown,
        row(0),
        row(1),
        g_qkv[None],
        row(2),
        row(3),
        g_proj[None],
        row(6),
        row(4),
        row(5),
        g_up[None],
        g_ub,
        g_down[None],
        row(7),
        rms,
    )


def solution(mesh):
    flat = P("section", None)
    deep = P("section", None, None)
    split = P("section", "dp", None, None)
    ranks = (flat, flat, deep, flat, flat, deep, flat, flat, flat, deep, flat, deep, flat)
    return jax.shard_map(
        functools.partial(per_device, mesh.shape["dp"]),
        mesh=mesh,
        in_specs=(split, P("dp"), P("section", "dp", None), *ranks),
        out_specs=(split, *ranks, flat),
        check_vma=False,
    )
```

```python
import functools

import jax
import jax.numpy as jnp
from jax import lax
from jax.experimental import pallas as pl
from jax.experimental.pallas import tpu as pltpu
from jax.sharding import PartitionSpec as P

HEADS = 12
CHUNKS = 16
TILE = 256
WIDE = 512
UNROLL = 2
KEEP_SCALE = 4.0 / 3.0
EPS = 1e-06
F32 = jnp.float32
BF16 = jnp.bfloat16
VMEM = pl.BlockSpec(memory_space=pltpu.VMEM)
SMEM = pl.BlockSpec(memory_space=pltpu.SMEM)
ANY = pl.BlockSpec(memory_space=pl.ANY)
HBM = pl.BlockSpec(memory_space=pltpu.HBM)
AG, AC, QB, VB, PB, MG, MC, DB, UB = range(9)


def dot_nn(left, right):
    return lax.dot_general(left, right, (((1,), (0,)), ((), ())), preferred_element_type=F32)


def dot_nt(left, right):
    return lax.dot_general(left, right, (((1,), (1,)), ((), ())), preferred_element_type=F32)


def dot_tn(left, right):
    return lax.dot_general(left, right, (((0,), (0,)), ((), ())), preferred_element_type=F32)


def shaped(*shape, dtype=BF16):
    return jax.ShapeDtypeStruct(shape, dtype)


def scratch(*shape, dtype=BF16):
    return pltpu.VMEM(shape, dtype)


def standardize(stream):
    centred = stream - jnp.mean(stream, axis=-1, keepdims=True)
    inverse = lax.rsqrt(jnp.mean(centred * centred, axis=-1, keepdims=True) + EPS)
    return centred * inverse, inverse


def norm_back(grad, normed, inverse):
    return inverse * (
        grad
        - jnp.mean(grad, axis=-1, keepdims=True)
        - normed * jnp.mean(grad * normed, axis=-1, keepdims=True)
    )


def lanes(start, size):
    return pl.ds(pl.multiple_of(start, 128), size)


def rows_at(start, size):
    return pl.ds(pl.multiple_of(start, 16), size)


def row_mask(length, valid):
    return lax.broadcasted_iota(jnp.int32, (length, 1), 0) < valid


class Copies:
    def __init__(self, sems):
        self.sems, self.used, self.out = sems, 0, []

    def start(self, src, dst):
        copy = pltpu.make_async_copy(src, dst, self.sems.at[self.used])
        self.used += 1
        copy.start()
        return copy

    def send(self, src, dst):
        self.out.append(self.start(src, dst))

    def finish(self):
        for copy in self.out:
            copy.wait()


def forward_kernel(image, skip, *refs):
    (act, valid, keep, vecs, x_in, qkvw_in, pw_in, uw_in, dw_in) = refs[:9]
    refs = refs[:9] + refs[9 + skip :]
    outs, stat, refs = refs[9:18], refs[18], refs[19:]
    (x, qkvw, pw, uw, dw, n1, qkv, probs, mixed, h1, n2, slope, gact, h2, sems) = refs
    (n1_out, qkv_out, probs_out, mixed_out, h1_out, n2_out, slope_out, gact_out, h2_out) = outs
    length, width = x.shape
    hidden = uw.shape[1]
    tiles = width // TILE
    low = lax.broadcasted_iota(jnp.int32, (1, 128), 1) < 64

    @pl.when(act[0] == 1)
    def _():
        copies = Copies(sems)
        get_x = copies.start(x_in, x)
        get_qkvw = copies.start(qkvw_in, qkvw)
        get_pw = copies.start(pw_in, pw)
        get_uw = copies.start(uw_in, uw)
        get_dw = copies.start(dw_in, dw)

        get_x.wait()
        normed, _inv = standardize(x[...].astype(F32))
        n1[...] = (normed * vecs[AG : AG + 1, :] + vecs[AC : AC + 1, :]).astype(BF16)
        copies.send(n1, n1_out)
        get_qkvw.wait()
        for part, bias in ((0, QB), (1, None), (2, VB)):
            for t in range(tiles):
                at = slice(part * width + t * TILE, part * width + (t + 1) * TILE)
                out = dot_nn(n1[...], qkvw[:, at])
                if bias is not None:
                    out = out + vecs[bias : bias + 1, t * TILE : (t + 1) * TILE]
                if part == 0:
                    out = out * 0.125
                qkv[:, at] = out.astype(BF16)
        copies.send(qkv, qkv_out)

        live = lax.broadcasted_iota(jnp.int32, (1, length), 1) < valid[image]

        def pair(p, _):
            q = qkv[:, lanes(p * 128, 128)]
            k = qkv[:, lanes(width + p * 128, 128)]
            v = qkv[:, lanes(2 * width + p * 128, 128)]
            zero = jnp.zeros_like(q)
            stacked = jnp.concatenate([jnp.where(low, q, zero), jnp.where(low, zero, q)], axis=0)
            scores = dot_nt(stacked, k)
            scores = jnp.where(live, scores, -1e30)
            top = jnp.max(scores, axis=-1, keepdims=True)
            e = jnp.exp(scores - top)
            total = jnp.sum(e, axis=-1, keepdims=True)
            prob = (e * (1.0 / total)).astype(BF16)
            probs[rows_at(p * 2 * length, 2 * length), :] = prob
            out = dot_nn(prob, v)
            mixed[:, lanes(p * 128, 128)] = jnp.where(low, out[:length], out[length:]).astype(BF16)
            return 0

        lax.fori_loop(0, width // 128, pair, 0, unroll=UNROLL)
        copies.send(probs, probs_out)
        copies.send(mixed, mixed_out)

        get_pw.wait()
        mask = row_mask(length, valid[image])
        a = keep[2 * image] * (dot_nn(mixed[...], pw[...]) + vecs[PB : PB + 1, :])
        stat[1] = jnp.sum(jnp.where(mask, a * a, 0.0))
        h = x[...].astype(F32) + a
        h1[...] = h
        normed, _inv = standardize(h)
        n2[...] = (normed * vecs[MG : MG + 1, :] + vecs[MC : MC + 1, :]).astype(BF16)
        copies.send(h1, h1_out)
        copies.send(n2, n2_out)

        get_uw.wait()

        def tile(t, _):
            at = lanes(t * TILE, TILE)
            ub = vecs[pl.ds(UB + t // tiles, 1), lanes((t % tiles) * TILE, TILE)]
            u = dot_nn(n2[...], uw[:, at]) + ub
            cdf = 0.5 * (1.0 + lax.erf(u * 0.7071067811865476))
            gact[:, at] = (u * cdf).astype(BF16)
            slope[:, at] = (cdf + u * (jnp.exp(-0.5 * u * u) * 0.3989422804014327)).astype(BF16)
            return 0

        lax.fori_loop(0, hidden // TILE, tile, 0, unroll=UNROLL)
        copies.send(gact, gact_out)
        copies.send(slope, slope_out)

        get_dw.wait()
        sum_h = 0.0
        sum_m = 0.0
        for t in range(tiles):
            at = slice(t * TILE, (t + 1) * TILE)
            m = keep[2 * image + 1] * (dot_nn(gact[...], dw[:, at]) + vecs[DB : DB + 1, at])
            h = h1[:, at] + m
            sum_h += jnp.sum(jnp.where(mask, h * h, 0.0))
            sum_m += jnp.sum(jnp.where(mask, m * m, 0.0))
            h2[:, at] = h.astype(BF16)
        stat[0] = sum_h
        stat[2] = sum_m
        copies.send(h2, h2_out)
        copies.finish()


def backward_kernel(image, skip, *refs):
    (act, keep, vecs, seed_in, dw_in, slope_in, uw_in, h1_in, pw_in) = refs[:9]
    (qkv_in, mixed_in, probs_in, x_in, qkvw_in) = refs[9:14]
    refs = refs[14 + skip :]
    (du_out, dy_out, dj_out, dx_out, vec) = refs[:5]
    (seed, dw, slope, uw, h1, pw, qkv, mixed, probs, x, qkvw, du, dy, dj, dx, dmix, dh1, sems) = refs[5:]
    length, width = x.shape
    hidden = uw.shape[1]
    low = lax.broadcasted_iota(jnp.int32, (1, 128), 1) < 64

    @pl.when(act[0] == 1)
    def _():
        copies = Copies(sems)
        get_seed = copies.start(seed_in, seed)
        get_dw = copies.start(dw_in, dw)
        get_slope = copies.start(slope_in, slope)
        get_uw = copies.start(uw_in, uw)
        get_h1 = copies.start(h1_in, h1)
        get_pw = copies.start(pw_in, pw)
        get = [
            copies.start(a, b) for a, b in ((qkv_in, qkv), (mixed_in, mixed), (probs_in, probs))
        ]
        get_x = copies.start(x_in, x)
        get_qkvw = copies.start(qkvw_in, qkvw)

        get_seed.wait()
        z = (keep[2 * image + 1] * seed[...].astype(F32)).astype(BF16)
        dx[...] = z
        vec[3:4, :] = jnp.sum(z.astype(F32), axis=0, keepdims=True)
        get_dw.wait()
        get_slope.wait()
        tiles = width // TILE

        def tile(t, _):
            at = lanes(t * TILE, TILE)
            d = dot_nt(dx[...], dw[rows_at(t * TILE, TILE), :])
            d = (d * slope[:, at].astype(F32)).astype(BF16)
            du[:, at] = d
            vec[pl.ds(4 + t // tiles, 1), lanes((t % tiles) * TILE, TILE)] = jnp.sum(
                d.astype(F32), axis=0, keepdims=True
            )
            return 0

        lax.fori_loop(0, hidden // TILE, tile, 0, unroll=UNROLL)
        copies.send(du, du_out)
        get_uw.wait()
        get_h1.wait()
        dn2 = dot_nt(du[...], uw[...])
        normed, inverse = standardize(h1[...])
        vec[1:2, :] = jnp.sum(dn2 * normed, axis=0, keepdims=True)
        vec[2:3, :] = jnp.sum(dn2, axis=0, keepdims=True)
        d = seed[...].astype(F32) + norm_back(dn2 * vecs[MG : MG + 1, :], normed, inverse)
        dh1[...] = d
        y = (keep[2 * image] * d).astype(BF16)
        dy[...] = y
        vec[0:1, :] = jnp.sum(y.astype(F32), axis=0, keepdims=True)
        copies.send(dy, dy_out)
        get_pw.wait()
        dmix[...] = dot_nt(dy[...], pw[...]).astype(BF16)
        for copy in get:
            copy.wait()

        def pair(p, _):
            at = lanes(p * 128, 128)
            k_at = lanes(width + p * 128, 128)
            v_at = lanes(2 * width + p * 128, 128)
            q = qkv[:, at]
            k = qkv[:, k_at]
            v = qkv[:, v_at]
            g = dmix[:, at]

            def stack(a):
                zero = jnp.zeros_like(a)
                return jnp.concatenate([jnp.where(low, a, zero), jnp.where(low, zero, a)], axis=0)

            both = stack(g)
            prod = g.astype(F32) * mixed[:, at].astype(F32)
            side = jnp.concatenate(
                [
                    jnp.sum(jnp.where(low, prod, 0.0), axis=-1, keepdims=True),
                    jnp.sum(jnp.where(low, 0.0, prod), axis=-1, keepdims=True),
                ],
                axis=0,
            )
            prob = probs[rows_at(p * 2 * length, 2 * length), :]
            dp = dot_nt(both, v)
            ds = (prob.astype(F32) * (dp - side)).astype(BF16)
            dj[:, v_at] = dot_tn(prob, both).astype(BF16)
            dq = dot_nn(ds, k)
            dj[:, at] = (0.125 * jnp.where(low, dq[:length], dq[length:])).astype(BF16)
            dj[:, k_at] = dot_tn(ds, stack(q)).astype(BF16)
            return 0

        lax.fori_loop(0, width // 128, pair, 0, unroll=UNROLL)
        copies.send(dj, dj_out)
        get_x.wait()
        get_qkvw.wait()
        vec[10:11, :] = jnp.sum(dj[:, 0:width].astype(F32), axis=0, keepdims=True)
        vec[11:12, :] = jnp.sum(dj[:, 2 * width :].astype(F32), axis=0, keepdims=True)
        dn1 = dot_nt(dj[...], qkvw[...])
        normed, inverse = standardize(x[...].astype(F32))
        vec[8:9, :] = jnp.sum(dn1 * normed, axis=0, keepdims=True)
        vec[9:10, :] = jnp.sum(dn1, axis=0, keepdims=True)
        d = dh1[...] + norm_back(dn1 * vecs[AG : AG + 1, :], normed, inverse)
        dx[...] = d.astype(BF16)
        copies.send(dx, dx_out)
        copies.finish()


def send_chunks(copies, code, full, pieces):
    rows = full.shape[1] // CHUNKS
    for ref, start in zip(pieces, (8, 4, 2, 1, 0)):
        for j in range(ref.shape[0]):
            which = jnp.bitwise_xor(code, start + j)
            copies.send(full.at[:, rows_at(which * rows, rows), :], ref.at[j])


def gather_rows(copies, ins, held):
    rows = ins[0].shape[0]
    return [
        copies.start(one, held.at[pl.ds(i * rows, rows), :]) for i, one in enumerate(ins)
    ]


def down_grad_kernel(images, skip, *refs):
    act, codes, keep, refs = *refs[:3], refs[3:]
    seed_in, gact_in, refs = refs[:images], refs[images : 2 * images], refs[2 * images + skip :]
    pieces, (dz, gact, full, sems) = refs[:5], refs[5:]

    @pl.when(act[0] == 1)
    def _():
        copies = Copies(sems)
        get = gather_rows(copies, seed_in, dz) + gather_rows(copies, gact_in, gact)
        for copy in get[:images]:
            copy.wait()
        length = dz.shape[0] // images
        for i in range(images):
            r = slice(i * length, (i + 1) * length)
            dz[r, :] = (keep[2 * i + 1] * dz[r, :].astype(F32)).astype(BF16)
        for copy in get[images:]:
            copy.wait()

        def tile(t, _):
            at = pl.multiple_of(t * WIDE, WIDE)
            full[0, pl.ds(at, WIDE), :] = dot_tn(gact[:, pl.ds(at, WIDE)], dz[...]).astype(BF16)
            return 0

        lax.fori_loop(0, gact.shape[1] // WIDE, tile, 0)
        send_chunks(copies, codes[0], full, pieces)
        copies.finish()


def up_grad_kernel(images, skip, *refs):
    act, codes, refs = *refs[:2], refs[2:]
    n = images
    ins, refs = [refs[k * n : (k + 1) * n] for k in range(2)], refs[2 * n + skip :]
    pieces, (n2, du, full, sems) = refs[:5], refs[5:]

    @pl.when(act[0] == 1)
    def _():
        copies = Copies(sems)
        get = [gather_rows(copies, i, h) for i, h in zip(ins, (n2, du))]
        tiles = full.shape[2] // TILE
        for copy in get[0] + get[1]:
            copy.wait()

        def tile(t, _):
            at = lanes(t * TILE, TILE)
            to = lanes((t % tiles) * TILE, TILE)
            full[t // tiles, :, to] = dot_tn(n2[...], du[:, at]).astype(BF16)
            return 0

        lax.fori_loop(0, du.shape[1] // TILE, tile, 0)
        send_chunks(copies, codes[1], full, pieces)
        copies.finish()


def qkv_grad_kernel(images, skip, *refs):
    act, codes, refs = *refs[:2], refs[2:]
    n = images
    ins, refs = [refs[k * n : (k + 1) * n] for k in range(4)], refs[4 * n + skip :]
    pieces, (n1, dj, mixed, dy, full, sems) = refs[:5], refs[5:]

    @pl.when(act[0] == 1)
    def _():
        copies = Copies(sems)
        get = [gather_rows(copies, i, h) for i, h in zip(ins, (n1, dj, mixed, dy))]
        tiles = full.shape[2] // TILE
        for copy in get[0] + get[1]:
            copy.wait()

        def tile(t, _):
            at = lanes(t * TILE, TILE)
            to = lanes((t % tiles) * TILE, TILE)
            full[t // tiles, :, to] = dot_tn(n1[...], dj[:, at]).astype(BF16)
            return 0

        lax.fori_loop(0, dj.shape[1] // TILE, tile, 0)
        for copy in get[2] + get[3]:
            copy.wait()
        full[full.shape[0] - 1] = dot_tn(mixed[...], dy[...]).astype(BF16)
        send_chunks(copies, codes[2], full, pieces)
        copies.finish()


def call(body, scalars, vecs, arrays, over, after, outs, held, copies, flops, limit):
    tail = [*after, *(o for o, _ in over)]
    ops = (*scalars, *vecs, *arrays, *tail)
    first = len(scalars) + len(vecs) + len(arrays) + len(after)

    def place(o):
        if o.shape == (8,):
            return SMEM
        return VMEM if o.dtype == F32 and o.shape[0] == 16 else HBM

    moved = sum(o.size * o.dtype.itemsize for o in arrays) + sum(o.size * o.dtype.itemsize for o in outs)
    return pl.pallas_call(
        body,
        out_shape=list(outs),
        in_specs=[SMEM] * len(scalars) + [VMEM] * len(vecs) + [ANY] * (len(arrays) + len(tail)),
        out_specs=[place(o) for o in outs],
        scratch_shapes=[*held, pltpu.SemaphoreType.DMA((copies,))],
        input_output_aliases={first + k: out for k, (_, out) in enumerate(over)},
        compiler_params=pltpu.CompilerParams(vmem_limit_bytes=limit << 20),
        cost_estimate=pl.CostEstimate(flops=int(flops), bytes_accessed=int(moved), transcendentals=0),
    )(*ops)


def piece_shapes(blocks, rows, width):
    return [shaped(n, blocks, rows, width) for n in (8, 4, 2, 1, 1)]


def like(*arrays):
    return [scratch(*a.shape, dtype=a.dtype) for a in arrays]


def forward(act, valid, keep, x, vecs, mats, image, after):
    qkvw, pw, uw, dw = mats
    length, width = x.shape
    hidden = uw.shape[1]
    thin, wide = shaped(length, width), shaped(length, hidden)
    outs = [
        thin,
        shaped(length, 3 * width),
        shaped(HEADS * length, length),
        thin,
        shaped(length, width, dtype=F32),
        thin,
        wide,
        wide,
        thin,
    ]
    *saved, h2, stat = call(
        functools.partial(forward_kernel, image, len(after)),
        (act, valid, keep),
        (vecs,),
        (x, qkvw, pw, uw, dw),
        (),
        after,
        [*outs, shaped(8, dtype=F32)],
        like(x, qkvw, pw, uw, dw, *outs),
        14,
        flops=2 * length * width * width * 14,
        limit=48,
    )
    return h2, stat, (x, *saved)


def backward(act, keep, seed, saved, vecs, mats, image, after):
    qkvw, pw, uw, dw = mats
    (x, n1, qkv, probs, mixed, h1, n2, slope, gact) = saved
    length, width = x.shape
    thin = shaped(length, width)
    outs = [slope, thin, qkv, thin]
    ins = (seed, dw, slope, uw, h1, pw, qkv, mixed, probs, x, qkvw)
    return call(
        functools.partial(backward_kernel, image, len(after)),
        (act, keep),
        (vecs,),
        ins,
        (),
        after,
        [*outs, shaped(16, width, dtype=F32)],
        like(*ins, *outs, thin, h1),
        15,
        flops=2 * length * width * width * 16,
        limit=48,
    )


def grads_call(body, scalars, groups, over, full, after):
    images = len(groups[0])
    length = groups[0][0].shape[0]
    held = [scratch(images * length, g[0].shape[1]) for g in groups]
    return call(
        functools.partial(body, images, len(over) + len(after)),
        scalars,
        (),
        [one for g in groups for one in g],
        over,
        after,
        piece_shapes(full[0], full[1] // CHUNKS, full[2]),
        [*held, scratch(*full)],
        len(groups) * images + CHUNKS,
        flops=2 * images * length * full[0] * full[1] * full[2],
        limit=48,
    )


def orders(bits):
    if bits == 4:
        return ((0, 1, 2, 3), (1, 2, 0, 3), (2, 0, 1, 3))
    plain = tuple(range(bits))
    return (plain, plain, plain)


def flipped(block, bit, sections, size):
    route = [(s * size + i, s * size + (i ^ (1 << bit))) for s in sections for i in range(size)]
    return lax.ppermute(block, ("section", "dp"), route)


def chunk_code(order, place):
    code = jnp.zeros((), jnp.int32)
    for k, bit in enumerate(order):
        code = code + (((place >> bit) & 1) << (len(order) - 1 - k))
    return code


STEPS = (
    (0, 1), (3, 0), (1, 1), (2, 1), (0, 2), (3, 1), (1, 2), (2, 2), (0, 3), (3, 2), (1, 3), (2, 3),
    (0, 4), (3, 3), (1, 4), (2, 4), (0, 5), (1, 5), (2, 5), (0, 6), (1, 6), (2, 6), (0, 7), (1, 7), (2, 7),
)


class Sum:
    def __init__(self, pieces, order, first):
        self.pieces, self.order, self.arrived, self.have = pieces, order, [first], None

    def send(self, step, after):
        if step < 5:
            count = 8 >> step
            parts = [self.pieces[step].astype(F32)]
            low = count if step < 4 else 0
            high = 2 * count if step < 4 else 1
            for r in self.arrived:
                parts.append(r[low:high].astype(F32))
            block = sum(parts[1:], parts[0]).astype(BF16)
        else:
            block = jnp.concatenate([self.have, self.last])
        block, _ = lax.optimization_barrier((block, after))
        return block

    def run(self, step, after, size):
        block = self.send(step, after)
        bit = self.order[step] if step < 4 else self.order[7 - step]
        got = flipped(block, bit, (0, 1), size)
        if step < 4:
            self.arrived.append(got)
        else:
            self.have, self.last = block, got
        return block


def settle(code, halves, blocks, shapes, after):
    _, _, rows, width = halves[0].shape

    def body(scalars, lower, upper, _, *outs):
        j = pl.program_id(0)
        for src, here in ((lower, j < 8), (upper, j >= 8)):

            @pl.when(here)
            def _(src=src):
                at = 0
                for count, out in zip(blocks, outs):
                    for b in range(count):
                        out[:, b * width : (b + 1) * width] = src[0, at].astype(F32)
                        at += 1

    block = (1, *halves[0].shape[1:])
    outs = [shaped(*s, dtype=F32) for s in shapes]
    return pl.pallas_call(
        body,
        out_shape=outs,
        grid_spec=pltpu.PrefetchScalarGridSpec(
            num_scalar_prefetch=1,
            grid=(CHUNKS,),
            in_specs=[
                pl.BlockSpec(block, lambda j, s: (jnp.minimum(j, 7), 0, 0, 0)),
                pl.BlockSpec(block, lambda j, s: (jnp.maximum(j - 8, 0), 0, 0, 0)),
                ANY,
            ],
            out_specs=[
                pl.BlockSpec((rows, count * width), lambda j, s: (jnp.bitwise_xor(s[0], j), 0))
                for count in blocks
            ],
        ),
        compiler_params=pltpu.CompilerParams(vmem_limit_bytes=16 << 20),
        cost_estimate=pl.CostEstimate(
            flops=0, bytes_accessed=sum(o.size * 6 for o in outs), transcendentals=0
        ),
    )(code.reshape(1), *halves, after)


def per_device(size, ends, counts, keep, *params):
    ag, ac, qkvw, qb, vb, pw, pb, mg, mc, uw, ub, dw, db = params
    mats = [item[0] for item in (qkvw, pw, uw, dw)]
    section = lax.axis_index("section")
    place = lax.axis_index("dp")
    first = section == 0
    images, slots, width = ends.shape[1:]
    hidden = ub.shape[1]
    blocks = hidden // width
    vecs = jnp.concatenate([ag, ac, qb, vb, pb, mg, mc, db, ub.reshape(blocks, width)])
    length = -(-slots // 32) * 32
    bits = size.bit_length() - 1
    ways = orders(bits)
    if size == CHUNKS:
        codes = [chunk_code(o, place) for o in ways]
    else:
        codes = [jnp.zeros((), jnp.int32)] * 3
    coded = jnp.stack(codes)
    acts = [(section == s).astype(jnp.int32).reshape(1) for s in (0, 1)]
    keeping = (keep[0].astype(F32) * KEEP_SCALE).reshape(-1)
    live = (jnp.arange(slots)[None, :] < counts[:, None])[..., None]

    def padded(block):
        return jnp.pad(block, ((0, length - slots), (0, 0)))

    def crossed(block, source):
        route = [(source * size + i, (1 - source) * size + i) for i in range(size)]
        return lax.ppermute(block, ("section", "dp"), route)

    every = range(images)
    early = size == CHUNKS
    acts_on = {0: acts[0], 1: acts[1]}
    token = []

    def forwards(which, xs):
        ran = []
        for i in every:
            ran.append(forward(acts_on[which], counts, keeping, xs[i], vecs, mats, i, list(token)))
            token[:] = [ran[-1][2][1]]
        return ran

    def backwards(which, seeds, kept, gates=()):
        back = []
        for i in every:
            after = [*token, *(gates if i == images - 1 else ())]
            back.append(backward(acts_on[which], keeping, seeds[i], kept[i], vecs, mats, i, after))
            token[:] = [back[-1][0]]
        return back

    def grads(kernel, which, groups, old, full):
        over = [(p, k) for k, p in enumerate(old) if k > 0 or not early]
        scalars = (acts_on[which], coded)
        if kernel is down_grad_kernel:
            scalars = (*scalars, keeping)
        pieces = grads_call(kernel, scalars, groups, over, full, list(token))
        token[:] = [pieces[0]]
        return pieces

    def column(kept, k):
        return [one[k] for one in kept]

    down_full, up_full, qkv_full = (1, hidden, width), (blocks, width, width), (4, width, width)

    x0 = [padded(ends[0, i]) for i in every]
    ran0 = forwards(0, x0)
    x1 = [crossed(ran0[i][0], 0) for i in every]
    ran1 = forwards(1, x1)
    kept0, kept1 = ([r[2] for r in ran] for ran in (ran0, ran1))

    def weight_grads(which, kept, back, old):
        pb = grads(up_grad_kernel, which, (column(kept, 6), column(back, 0)), old[0], up_full)
        sources = (column(kept, 1), column(back, 2), column(kept, 4), column(back, 1))
        pc = grads(qkv_grad_kernel, which, sources, old[1], qkv_full)
        return pb, pc

    seed1 = [padded(jnp.where(live[i], ends[0, i], jnp.zeros((), BF16))) for i in every]
    pa1 = grads(down_grad_kernel, 1, (seed1, column(kept1, 8)), (), down_full)
    gates = ()
    if early:
        ra1 = flipped(pa1[0], ways[0][0], (1,), size)
        gates = (ra1,)
    back1 = backwards(1, seed1, kept1, gates)
    seed0 = [crossed(back1[i][3], 1) for i in every]
    pb1, pc1 = weight_grads(1, kept1, back1, ((), ()))
    if early:
        rb1 = flipped(pb1[0], ways[1][0], (1,), size)
        rc1 = flipped(pc1[0], ways[2][0], (1,), size)
    back0 = backwards(0, seed0, kept0)
    pa = grads(down_grad_kernel, 0, (seed0, column(kept0, 8)), pa1, down_full)
    pb, pc = weight_grads(0, kept0, back0, (pb1, pc1))

    def both(a, b):
        return jnp.where(first, sum(a[1:], a[0]), sum(b[1:], b[0]))

    made = both(column(back0, 4), column(back1, 4))
    stats = both(column(ran0, 1), column(ran1, 1))[:3]
    extra = jnp.concatenate([stats, jnp.sum(counts.astype(F32)).reshape(1)])
    extra = jnp.pad(extra, (0, width - 4)).reshape(1, width)
    vec = jnp.concatenate([made[:12], extra])

    if early:
        sums = []
        for p, one, way in zip((pa, pb, pc), (ra1, rb1, rc1), ways):
            got = flipped(p[0], way[0], (0,), size)
            sums.append(Sum(p, way, jnp.where(first, got, one)))
        after = pc[4]
        for which, step in STEPS:
            if which == 3:
                vec, _ = lax.optimization_barrier((vec, after))
                after = vec
                vec = vec + flipped(vec, step, (0, 1), size)
            else:
                after = sums[which].run(step, after, size)
        halves = [(s.have, s.last) for s in sums]
    else:
        halves = []
        for p in (pa, pb, pc):
            whole = lax.psum(jnp.concatenate(p[::-1]), "dp")
            halves.append((whole[:8], whole[8:]))
        for bit in range(bits):
            vec = vec + flipped(vec, bit, (0, 1), size)
        after = vec

    (g_down,) = settle(codes[0], halves[0], (1,), [(hidden, width)], after)
    g_qkv, g_proj = settle(
        codes[2], halves[2], (3, 1), [(width, 3 * width), (width, width)], g_down
    )
    (g_up,) = settle(codes[1], halves[1], (blocks,), [(width, hidden)], g_qkv)

    shown = jnp.stack([jnp.where(first, back0[i][3], ran1[i][0])[:slots] for i in every])
    shown = jnp.where(live, shown, jnp.zeros((), BF16))[None]
    rms = jnp.sqrt(vec[-1, 0:3] / (vec[-1, 3] * width)).reshape(1, 3)
    row = lambda k: vec[k : k + 1]
    return (
        shown,
        row(8),
        row(9),
        g_qkv[None],
        row(10),
        row(11),
        g_proj[None],
        row(0),
        row(1),
        row(2),
        g_up[None],
        vec[4 : 4 + blocks].reshape(1, hidden),
        g_down[None],
        row(3),
        rms,
    )


def solution(mesh):
    flat = P("section", None)
    deep = P("section", None, None)
    split = P("section", "dp", None, None)
    ranks = (flat, flat, deep, flat, flat, deep, flat, flat, flat, deep, flat, deep, flat)
    return jax.shard_map(
        functools.partial(per_device, mesh.shape["dp"]),
        mesh=mesh,
        in_specs=(split, P("dp"), P("section", "dp", None), *ranks),
        out_specs=(split, *ranks, flat),
        check_vma=False,
    )
```

```python
import functools

import jax
import jax.numpy as jnp
from jax import lax
from jax.experimental import pallas as pl
from jax.experimental.pallas import tpu as pltpu
from jax.sharding import PartitionSpec as P

HEADS = 12
CHUNKS = 16
PARTS = 2
TILE = 768
UNROLL = 2
KEEP_SCALE = 4.0 / 3.0
EPS = 1e-06
F32 = jnp.float32
BF16 = jnp.bfloat16
VMEM = pl.BlockSpec(memory_space=pltpu.VMEM)
SMEM = pl.BlockSpec(memory_space=pltpu.SMEM)
ANY = pl.BlockSpec(memory_space=pl.ANY)
HBM = pl.BlockSpec(memory_space=pltpu.HBM)
AG, AC, QB, VB, PB, MG, MC, DB, UB = range(9)
NONE = 15


def dot_nn(left, right):
    return lax.dot_general(left, right, (((1,), (0,)), ((), ())), preferred_element_type=F32)


def dot_nt(left, right):
    return lax.dot_general(left, right, (((1,), (1,)), ((), ())), preferred_element_type=F32)


def dot_tn(left, right):
    return lax.dot_general(left, right, (((0,), (0,)), ((), ())), preferred_element_type=F32)


def shaped(*shape, dtype=BF16):
    return jax.ShapeDtypeStruct(shape, dtype)


def scratch(*shape, dtype=BF16):
    return pltpu.VMEM(shape, dtype)


def standardize(stream):
    centred = stream - jnp.mean(stream, axis=-1, keepdims=True)
    inverse = lax.rsqrt(jnp.mean(centred * centred, axis=-1, keepdims=True) + EPS)
    return centred * inverse, inverse


def norm_back(grad, normed, inverse):
    return inverse * (
        grad
        - jnp.mean(grad, axis=-1, keepdims=True)
        - normed * jnp.mean(grad * normed, axis=-1, keepdims=True)
    )


def lanes(start, size):
    return pl.ds(pl.multiple_of(start, 128), size)


def rows_at(start, size):
    return pl.ds(pl.multiple_of(start, 16), size)


def row_mask(length, valid):
    return lax.broadcasted_iota(jnp.int32, (length, 1), 0) < valid


class Copies:
    def __init__(self, sems):
        self.sems, self.used, self.out = sems, 0, []

    def start(self, src, dst):
        copy = pltpu.make_async_copy(src, dst, self.sems.at[self.used])
        self.used += 1
        copy.start()
        return copy

    def send(self, src, dst):
        self.out.append(self.start(src, dst))

    def finish(self):
        for copy in self.out:
            copy.wait()


def loading_forward_kernel(image, *refs):
    (act, valid, keep, ag, ac, qb, vb, pb, mg, mc, db, ub, *mats_in, x_in) = refs[:17]
    outs, vecs, mats, rest = refs[17:27], refs[27], refs[28:32], refs[32:]
    *rest, mat_sems = rest
    gets = [
        pltpu.make_async_copy(a, b, mat_sems.at[i]) for i, (a, b) in enumerate(zip(mats_in, mats))
    ]
    for get in gets:
        get.start()
    width = vecs.shape[1]
    for k, one in enumerate((ag, ac, qb, vb, pb, mg, mc, db)):
        vecs[k : k + 1, :] = one[...]
    vecs[NONE : NONE + 1, :] = jnp.zeros((1, width), F32)
    for k in range(ub.shape[1] // width):
        vecs[UB + k : UB + k + 1, :] = ub[:, k * width : (k + 1) * width]

    @pl.when(act[0] == 0)
    def _():
        for get in gets:
            get.wait()

    forward_kernel(image, 0, gets, act, valid, keep, vecs, *mats, x_in, *outs, *rest)


def forward_kernel(image, skip, gets, *refs):
    (act, valid, keep, vecs, qkvw, pw, uw, dw, x_in) = refs[:9]
    refs = refs[:9] + refs[9 + skip :]
    outs, stat, refs = refs[9:18], refs[18], refs[19:]
    (x, n1, qkv, probs, mixed, h1, n2, slope, gact, h2, sems) = refs
    (n1_out, qkv_out, probs_out, mixed_out, h1_out, n2_out, slope_out, gact_out, h2_out) = outs
    length, width = x.shape
    hidden = uw.shape[1]
    tiles = width // TILE
    low = lax.broadcasted_iota(jnp.int32, (1, 128), 1) < 64

    @pl.when(act[0] == 1)
    def _():
        copies = Copies(sems)
        get_x = copies.start(x_in, x)

        get_x.wait()
        normed, _inv = standardize(x[...].astype(F32))
        n1[...] = (normed * vecs[AG : AG + 1, :] + vecs[AC : AC + 1, :]).astype(BF16)
        copies.send(n1, n1_out)
        if gets:
            gets[0].wait()

        def project(t, _):
            part = t // tiles
            at = lanes(t * TILE, TILE)
            bias = jnp.where(part == 0, QB, jnp.where(part == 1, NONE, VB))
            out = dot_nn(n1[...], qkvw[:, at])
            out = out + vecs[pl.ds(bias, 1), lanes((t - part * tiles) * TILE, TILE)]
            qkv[:, at] = (out * jnp.where(part == 0, 0.125, 1.0)).astype(BF16)
            return 0

        lax.fori_loop(0, 3 * tiles, project, 0)
        copies.send(qkv, qkv_out)

        live = lax.broadcasted_iota(jnp.int32, (1, length), 1) < valid[image]

        def pair(p, _):
            q = qkv[:, lanes(p * 128, 128)]
            k = qkv[:, lanes(width + p * 128, 128)]
            v = qkv[:, lanes(2 * width + p * 128, 128)]
            zero = jnp.zeros_like(q)
            stacked = jnp.concatenate([jnp.where(low, q, zero), jnp.where(low, zero, q)], axis=0)
            scores = dot_nt(stacked, k)
            scores = jnp.where(live, scores, -1e30)
            top = jnp.max(scores, axis=-1, keepdims=True)
            e = jnp.exp(scores - top)
            total = jnp.sum(e, axis=-1, keepdims=True)
            prob = (e * (1.0 / total)).astype(BF16)
            probs[rows_at(p * 2 * length, 2 * length), :] = prob
            out = dot_nn(prob, v)
            mixed[:, lanes(p * 128, 128)] = jnp.where(low, out[:length], out[length:]).astype(BF16)
            return 0

        lax.fori_loop(0, width // 128, pair, 0, unroll=UNROLL)
        copies.send(probs, probs_out)
        copies.send(mixed, mixed_out)

        mask = row_mask(length, valid[image])
        if gets:
            gets[1].wait()
            gets[2].wait()

        def attend_out(t, total):
            at = lanes(t * TILE, TILE)
            a = keep[2 * image] * (dot_nn(mixed[...], pw[:, at]) + vecs[PB : PB + 1, at])
            h1[:, at] = x[:, at].astype(F32) + a
            return total + jnp.sum(jnp.where(mask, a * a, 0.0))

        stat[1] = lax.fori_loop(0, tiles, attend_out, 0.0)
        normed, _inv = standardize(h1[...])
        n2[...] = (normed * vecs[MG : MG + 1, :] + vecs[MC : MC + 1, :]).astype(BF16)
        copies.send(h1, h1_out)
        copies.send(n2, n2_out)


        for block in range(hidden // width):

            def tile(t, _, block=block):
                at = lanes(block * width + t * TILE, TILE)
                u = dot_nn(n2[...], uw[:, at]) + vecs[UB + block : UB + block + 1, lanes(t * TILE, TILE)]
                cdf = 0.5 * (1.0 + lax.erf(u * 0.7071067811865476))
                gact[:, at] = (u * cdf).astype(BF16)
                slope[:, at] = (cdf + u * (jnp.exp(-0.5 * u * u) * 0.3989422804014327)).astype(BF16)
                return 0

            lax.fori_loop(0, tiles, tile, 0)
            at = slice(block * width, (block + 1) * width)
            copies.send(gact.at[:, at], gact_out.at[:, at])
            copies.send(slope.at[:, at], slope_out.at[:, at])

        if gets:
            gets[3].wait()

        def down(t, total):
            at = lanes(t * TILE, TILE)
            m = keep[2 * image + 1] * (dot_nn(gact[...], dw[:, at]) + vecs[DB : DB + 1, at])
            h = h1[:, at] + m
            h2[:, at] = h.astype(BF16)
            return (
                total[0] + jnp.sum(jnp.where(mask, h * h, 0.0)),
                total[1] + jnp.sum(jnp.where(mask, m * m, 0.0)),
            )

        stat[0], stat[2] = lax.fori_loop(0, tiles, down, (0.0, 0.0))
        copies.send(h2, h2_out)
        copies.finish()


def backward_kernel(image, skip, *refs):
    (act, valid, keep, vecs, dw, uw, pw, qkvw) = refs[:8]
    (seed_in, slope_in, h1_in, qkv_in, mixed_in, probs_in, x_in) = refs[8:15]
    refs = refs[15 + skip :]
    (du_out, dy_out, dj_out, dx_out, vec) = refs[:5]
    (seed, slope, h1, qkv, mixed, probs, x, du, dy, dj, dx, dmix, dh1, wide, sems) = refs[5:]
    length, width = x.shape
    hidden = uw.shape[1]
    low = lax.broadcasted_iota(jnp.int32, (1, 128), 1) < 64

    @pl.when(act[0] == 1)
    def _():
        copies = Copies(sems)
        get_seed = copies.start(seed_in, seed)
        get_slope = copies.start(slope_in, slope)
        get_h1 = copies.start(h1_in, h1)
        get = [
            copies.start(a, b) for a, b in ((qkv_in, qkv), (mixed_in, mixed), (probs_in, probs))
        ]
        get_x = copies.start(x_in, x)

        get_seed.wait()
        given = jnp.where(row_mask(length, valid[image]), seed[...].astype(F32), 0.0)
        z = (keep[2 * image + 1] * given).astype(BF16)
        dx[...] = z
        vec[3:4, :] = jnp.sum(z.astype(F32), axis=0, keepdims=True)
        get_slope.wait()
        tiles = width // TILE

        def tile(t, _):
            at = lanes(t * TILE, TILE)
            d = dot_nt(dx[...], dw[rows_at(t * TILE, TILE), :])
            d = (d * slope[:, at].astype(F32)).astype(BF16)
            du[:, at] = d
            vec[pl.ds(4 + t // tiles, 1), lanes((t % tiles) * TILE, TILE)] = jnp.sum(
                d.astype(F32), axis=0, keepdims=True
            )
            return 0

        lax.fori_loop(0, hidden // TILE, tile, 0)
        copies.send(du, du_out)
        get_h1.wait()

        def up_in(t, _):
            wide[:, lanes(t * TILE, TILE)] = dot_nt(du[...], uw[rows_at(t * TILE, TILE), :])
            return 0

        lax.fori_loop(0, tiles, up_in, 0)
        dn2 = wide[...]
        normed, inverse = standardize(h1[...])
        vec[1:2, :] = jnp.sum(dn2 * normed, axis=0, keepdims=True)
        vec[2:3, :] = jnp.sum(dn2, axis=0, keepdims=True)
        given = jnp.where(row_mask(length, valid[image]), seed[...].astype(F32), 0.0)
        d = given + norm_back(dn2 * vecs[MG : MG + 1, :], normed, inverse)
        dh1[...] = d
        y = (keep[2 * image] * d).astype(BF16)
        dy[...] = y
        vec[0:1, :] = jnp.sum(y.astype(F32), axis=0, keepdims=True)
        copies.send(dy, dy_out)

        def mix_in(t, _):
            dmix[:, lanes(t * TILE, TILE)] = dot_nt(dy[...], pw[rows_at(t * TILE, TILE), :]).astype(BF16)
            return 0

        lax.fori_loop(0, tiles, mix_in, 0)
        for copy in get:
            copy.wait()

        def pair(p, _):
            at = lanes(p * 128, 128)
            k_at = lanes(width + p * 128, 128)
            v_at = lanes(2 * width + p * 128, 128)
            q = qkv[:, at]
            k = qkv[:, k_at]
            v = qkv[:, v_at]
            g = dmix[:, at]

            def stack(a):
                zero = jnp.zeros_like(a)
                return jnp.concatenate([jnp.where(low, a, zero), jnp.where(low, zero, a)], axis=0)

            both = stack(g)
            prod = g.astype(F32) * mixed[:, at].astype(F32)
            side = jnp.concatenate(
                [
                    jnp.sum(jnp.where(low, prod, 0.0), axis=-1, keepdims=True),
                    jnp.sum(jnp.where(low, 0.0, prod), axis=-1, keepdims=True),
                ],
                axis=0,
            )
            prob = probs[rows_at(p * 2 * length, 2 * length), :]
            dp = dot_nt(both, v)
            ds = (prob.astype(F32) * (dp - side)).astype(BF16)
            dj[:, v_at] = dot_tn(prob, both).astype(BF16)
            dq = dot_nn(ds, k)
            dj[:, at] = (0.125 * jnp.where(low, dq[:length], dq[length:])).astype(BF16)
            dj[:, k_at] = dot_tn(ds, stack(q)).astype(BF16)
            return 0

        lax.fori_loop(0, width // 128, pair, 0, unroll=UNROLL)
        copies.send(dj, dj_out)
        get_x.wait()
        vec[10:11, :] = jnp.sum(dj[:, 0:width].astype(F32), axis=0, keepdims=True)
        vec[11:12, :] = jnp.sum(dj[:, 2 * width :].astype(F32), axis=0, keepdims=True)

        def stream_in(t, _):
            wide[:, lanes(t * TILE, TILE)] = dot_nt(dj[...], qkvw[rows_at(t * TILE, TILE), :])
            return 0

        lax.fori_loop(0, tiles, stream_in, 0)
        dn1 = wide[...]
        normed, inverse = standardize(x[...].astype(F32))
        vec[8:9, :] = jnp.sum(dn1 * normed, axis=0, keepdims=True)
        vec[9:10, :] = jnp.sum(dn1, axis=0, keepdims=True)
        d = dh1[...] + norm_back(dn1 * vecs[AG : AG + 1, :], normed, inverse)
        dx[...] = d.astype(BF16)
        copies.send(dx, dx_out)
        copies.finish()


def grad_kernel(kind, images, skip, *refs):
    section, codes, valid, keep, refs = *refs[:4], refs[4:]
    groups = {0: 2, 1: 2, 2: 4}[kind]
    n = images
    ins = [refs[k * n : (k + 1) * n] for k in range(2 * groups)]
    refs = refs[2 * groups * n + skip :]
    lower, upper = refs[:PARTS], refs[PARTS : 2 * PARTS]
    thin, wide, full, sems = refs[2 * PARTS :]
    blocks, width, _ = full.shape
    rows = lower[0].shape[1]
    per = width // (rows * PARTS)
    length = ins[0][0].shape[0]
    copies = Copies(sems)

    def load(group, to, at=slice(None)):
        gets = []
        for i in range(images):
            both = [
                pltpu.make_async_copy(
                    ins[s * groups + group][i].at[:, at],
                    to.at[pl.ds(i * length, length), :],
                    sems.at[copies.used],
                )
                for s in (0, 1)
            ]
            copies.used += 1
            pl.when(section[0] == 0)(both[0].start)
            pl.when(section[0] == 1)(both[1].start)
            gets.append(both[0])
        return gets

    def column(b):
        return slice(b * width, (b + 1) * width)

    get_thin = load(0, thin.at[0])
    tail = 1 if kind == 2 else 0
    get_wide = [load(1, wide.at[b], column(b)) for b in range(blocks - tail)]
    if tail:
        get_thin_2 = load(2, thin.at[1])
        get_wide.append(get_thin_2 + load(3, wide.at[blocks - 1]))
    for get in get_thin:
        get.wait()
    if kind == 0:
        for i in range(images):
            r = slice(i * length, (i + 1) * length)
            z = jnp.where(row_mask(length, valid[i]), thin[0, r, :].astype(F32), 0.0)
            thin[0, r, :] = (keep[2 * i + 1] * z).astype(BF16)
    for b in range(blocks):
        for get in get_wide[b]:
            get.wait()
        which = 1 if tail and b == blocks - 1 else 0

        def tile(t, _, b=b, which=which):
            at = lanes(t * TILE, TILE)
            if kind == 0:
                full[b, rows_at(t * TILE, TILE), :] = dot_tn(wide[b, :, at], thin[0]).astype(BF16)
            else:
                full[b, :, at] = dot_tn(thin[which], wide[b, :, at]).astype(BF16)
            return 0

        lax.fori_loop(0, width // TILE, tile, 0)

        for c in range(per * PARTS):
            part = c % PARTS
            place = jnp.bitwise_xor(codes[kind * PARTS + part], b * per + c // PARTS)
            source = full.at[b, c * rows : (c + 1) * rows, :]
            sem = sems.at[copies.used]
            copies.used += 1

            @pl.when(place < CHUNKS // 2)
            def _(source=source, to=lower[part], place=place, sem=sem):
                pltpu.make_async_copy(source, to.at[place], sem).start()

            @pl.when(place >= CHUNKS // 2)
            def _(source=source, to=upper[part], place=place, sem=sem):
                pltpu.make_async_copy(source, to.at[place - CHUNKS // 2], sem).start()

            copies.out.append(pltpu.make_async_copy(source, lower[part].at[0], sem))
    copies.finish()


def call(body, scalars, vecs, arrays, over, after, outs, held, copies, flops, limit):
    tail = [*after, *(o for o, _ in over)]
    ops = (*scalars, *vecs, *(held_in(pltpu.HBM, a) for a in (*arrays, *tail)))
    first = len(scalars) + len(vecs) + len(arrays) + len(after)

    def place(o):
        if isinstance(o, pl.MemoryRef):
            return VMEM
        if o.shape == (8,):
            return SMEM
        return VMEM if o.dtype == F32 and o.shape[0] == 16 else HBM

    moved = sum(o.size * o.dtype.itemsize for o in arrays)
    return pl.pallas_call(
        body,
        out_shape=[pltpu.HBM(o.shape, o.dtype) if place(o) is HBM else o for o in outs],
        in_specs=[SMEM] * len(scalars) + [VMEM] * len(vecs) + [HBM] * (len(arrays) + len(tail)),
        out_specs=[place(o) for o in outs],
        scratch_shapes=[*held, pltpu.SemaphoreType.DMA((copies,))],
        input_output_aliases={first + k: out for k, (_, out) in enumerate(over)},
        compiler_params=pltpu.CompilerParams(vmem_limit_bytes=limit << 20),
        cost_estimate=pl.CostEstimate(flops=int(flops), bytes_accessed=int(moved), transcendentals=0),
    )(*ops)


def held_in(space, array):
    return pltpu.with_memory_space_constraint(array, space)


def like(*arrays):
    return [scratch(*a.shape, dtype=a.dtype) for a in arrays]


def forward(act, valid, keep, x, vecs, mats, image, after, load=False):
    qkvw, pw, uw, dw = mats
    length, width = x.shape
    hidden = uw.shape[1]
    thin, wide = shaped(length, width), shaped(length, hidden)
    outs = [
        thin,
        shaped(length, 3 * width),
        shaped(HEADS * length, length),
        thin,
        shaped(length, width, dtype=F32),
        thin,
        wide,
        wide,
        thin,
    ]
    held = like(x, *outs)
    stat = shaped(8, dtype=F32)
    copies = 8 + 2 * hidden // width
    flops = 2 * length * width * width * 14
    if load:
        loaded = [stat, shaped(16, width, dtype=F32), *(pltpu.VMEM(m.shape, m.dtype) for m in mats)]
        got = call(
            functools.partial(loading_forward_kernel, image),
            (act, valid, keep),
            vecs,
            (qkvw, pw, uw, dw, x),
            (),
            (),
            [*outs, *loaded],
            [*held, pltpu.SemaphoreType.DMA((copies,))],
            len(mats),
            flops=flops,
            limit=36,
        )
        return got[8], got[9], (x, *got[:8]), got[10], [held_in(pltpu.VMEM, m) for m in got[11:]]
    *saved, h2, stat = call(
        functools.partial(forward_kernel, image, len(after), ()),
        (act, valid, keep),
        (vecs, qkvw, pw, uw, dw),
        (x,),
        (),
        after,
        [*outs, stat],
        held,
        copies,
        flops=flops,
        limit=36,
    )
    return h2, stat, (x, *saved)


def backward(act, valid, keep, seed, saved, vecs, mats, image, after):
    qkvw, pw, uw, dw = mats
    (x, n1, qkv, probs, mixed, h1, n2, slope, gact) = saved
    length, width = x.shape
    thin = shaped(length, width)
    outs = [slope, thin, qkv, thin]
    ins = (seed, slope, h1, qkv, mixed, probs, x)
    return call(
        functools.partial(backward_kernel, image, len(after)),
        (act, valid, keep),
        (vecs, dw, uw, pw, qkvw),
        ins,
        (),
        after,
        [*outs, shaped(16, width, dtype=F32)],
        like(*ins, *outs, thin, h1, h1),
        11,
        flops=2 * length * width * width * 16,
        limit=36,
    )


def weight_grad(kind, scalars, groups, width, after):
    images = len(groups[0])
    length = groups[0][0].shape[0]
    total = images * length
    held = [scratch(2 if kind == 2 else 1, total, width), scratch(4, total, width)]
    half = shaped(CHUNKS // 2, 4 * width // (CHUNKS * PARTS), width)
    got = call(
        functools.partial(grad_kernel, kind, images, len(after)),
        scalars,
        (),
        [one for g in groups for one in g],
        (),
        after,
        [half] * (2 * PARTS),
        [*held, scratch(4, width, width)],
        (5 if kind < 2 else 6) * images + CHUNKS * PARTS,
        flops=2 * images * length * 4 * width * width,
        limit=36,
    )
    return list(zip(got[:PARTS], got[PARTS:]))


def orders(bits):
    if bits == 4:
        return (
            ((0, 1, 2, 3), (0, 1, 2, 3)),
            ((1, 0, 2, 3), (2, 0, 1, 3)),
            ((0, 2, 1, 3), (2, 3, 0, 1)),
            ((1, 0, 2, 3), (1, 0, 2, 3)),
            ((2, 0, 1, 3), (2, 0, 1, 3)),
            ((1, 0, 2, 3), (0, 1, 2, 3)),
        )
    plain = (tuple(range(bits)),) * 2
    return (plain,) * (3 * PARTS)


def flipped(block, bits, sections, size):
    route = [(s * size + i, s * size + (i ^ (1 << bits[s]))) for s in sections for i in range(size)]
    return lax.ppermute(block, ("section", "dp"), route)


def chunk_code(order, place):
    code = jnp.zeros((), jnp.int32)
    for k, bit in enumerate(order):
        code = code + (((place >> bit) & 1) << (len(order) - 1 - k))
    return code


STEPS = (
    (2, 1), (1, 1), (3, 1), (0, 1), (6, 0), (3, 2), (1, 2), (0, 2), (3, 3), (5, 1), (1, 3), (6, 1),
    (2, 2), (0, 3), (4, 1), (1, 4), (5, 2), (0, 4), (6, 2), (3, 4), (1, 5), (4, 2), (2, 3), (3, 5),
    (4, 3), (6, 3), (1, 6), (0, 5), (5, 3), (2, 4), (3, 6), (0, 6), (4, 4), (5, 4), (1, 7), (0, 7),
    (2, 5), (5, 5), (4, 5), (2, 6), (3, 7), (4, 6), (2, 7), (5, 6), (4, 7), (5, 7),
)


class Sum:
    def __init__(self, lower, order, first):
        self.lower, self.order, self.arrived, self.have = lower, order, [first], None

    def send(self, step, after):
        if step < 5:
            low, high = (8 >> step, 16 >> step) if step < 4 else (0, 1)
            parts = [a[low:high].astype(F32) for a in (self.lower, *self.arrived)]
            block = sum(parts[1:], parts[0]).astype(BF16)
        else:
            block = jnp.concatenate([self.have, self.last])
        block, _ = lax.optimization_barrier((block, after))
        return block

    def run(self, step, after, size):
        block = self.send(step, after)
        bits = [o[step] if step < 4 else o[7 - step] for o in self.order]
        got = flipped(block, bits, (0, 1), size)
        if step < 4:
            self.arrived.append(got)
        else:
            self.have, self.last = block, got
        return block


def settle_kernel(kind, start, skip, code, *refs):
    halves, refs = refs[:PARTS], refs[PARTS + skip :]
    outs, (wide, sems) = refs[:-2], refs[-2:]
    count, rows, width = halves[0].shape
    waits = []
    for part, half in enumerate(halves):
        for k in range(count):
            slot = part * count + k
            wide[slot] = half[k].astype(F32)
            chunk = jnp.bitwise_xor(code[part], start + k)
            row = (chunk * PARTS + part) * rows
            block = row // width
            sem = sems.at[slot]
            if kind == 0:
                to = outs[0].at[pl.ds(pl.multiple_of(row, 8), rows), :]
                pltpu.make_async_copy(wide.at[slot], to, sem).start()
            else:
                at = pl.ds(pl.multiple_of(row - block * width, 8), rows)
                blocks = outs[0].shape[1] // width

                def first(slot=slot, at=at, block=block, sem=sem):
                    to = outs[0].at[at, pl.ds(pl.multiple_of(block * width, 128), width)]
                    pltpu.make_async_copy(wide.at[slot], to, sem).start()

                def second(slot=slot, at=at, sem=sem):
                    pltpu.make_async_copy(wide.at[slot], outs[1].at[at, :], sem).start()

                if kind == 1:
                    first()
                else:
                    pl.when(block < blocks)(first)
                    pl.when(block >= blocks)(second)
            waits.append(pltpu.make_async_copy(wide.at[slot], outs[0].at[0:rows, 0:width], sem))
    for wait in waits:
        wait.wait()


def settle(kind, start, codes, halves, outs, over):
    count, rows, width = halves[0].shape
    return pl.pallas_call(
        functools.partial(settle_kernel, kind, start, len(over)),
        out_shape=[pltpu.HBM(o.shape, F32) for o in outs],
        in_specs=[SMEM] + [VMEM] * PARTS + [HBM] * len(over),
        out_specs=[HBM] * len(outs),
        scratch_shapes=[
            scratch(PARTS * count, rows, width, dtype=F32),
            pltpu.SemaphoreType.DMA((PARTS * count,)),
        ],
        input_output_aliases={1 + PARTS + k: k for k in range(len(over))},
        compiler_params=pltpu.CompilerParams(vmem_limit_bytes=16 << 20),
    )(jnp.stack(codes), *halves, *(held_in(pltpu.HBM, o) for o in over))


def per_device(size, ends, counts, keep, *params):
    ag, ac, qkvw, qb, vb, pw, pb, mg, mc, uw, ub, dw, db = params
    mats = [item[0] for item in (qkvw, pw, uw, dw)]
    section = lax.axis_index("section")
    place = lax.axis_index("dp")
    first = section == 0
    images, slots, width = ends.shape[1:]
    hidden = ub.shape[1]
    blocks = hidden // width
    vecs = (ag, ac, qb, vb, pb, mg, mc, db, ub)
    length = -(-slots // 32) * 32
    bits = size.bit_length() - 1
    ways = orders(bits)
    starts = [[o[0] for o in way] for way in ways]
    if size == CHUNKS:
        codes = [jnp.where(first, *(chunk_code(o, place) for o in way)) for way in ways]
    else:
        codes = [jnp.zeros((), jnp.int32)] * (3 * PARTS)
    coded = jnp.stack(codes)
    acts = [(section == s).astype(jnp.int32).reshape(1) for s in (0, 1)]
    keeping = (keep[0].astype(F32) * KEEP_SCALE).reshape(-1)
    live = (jnp.arange(slots)[None, :] < counts[:, None])[..., None]

    def padded(block):
        return jnp.pad(block, ((0, length - slots), (0, 0)))

    def crossed(block, source):
        route = [(source * size + i, (1 - source) * size + i) for i in range(size)]
        return lax.ppermute(block, ("section", "dp"), route)

    every = range(images)
    early = size == CHUNKS
    acts_on = {0: acts[0], 1: acts[1]}
    token = []

    def forwards(which, xs, start):
        ran = list(start)
        for i in range(len(ran), images):
            ran.append(forward(acts_on[which], counts, keeping, xs[i], vecs, mats, i, list(token)))
            token[:] = [ran[-1][2][1]]
        return ran

    def backwards(which, seeds, kept):
        back = []
        for i in every:
            back.append(
                backward(acts_on[which], counts, keeping, seeds[i], kept[i], vecs, mats, i, list(token))
            )
            token[:] = [back[-1][0]]
        return back

    def grads(kind, *groups):
        scalars = (section.astype(jnp.int32).reshape(1), coded, counts, keeping)
        halves = weight_grad(kind, scalars, groups, width, list(token))
        token[:] = [halves[0][0]]
        return halves

    def column(kept, k):
        return [one[k] for one in kept]

    x0 = [padded(ends[0, i]) for i in every]
    *one, vecs, mats = forward(acts[0], counts, keeping, x0[0], vecs, mats, 0, (), True)
    token[:] = [one[2][1]]
    ran0 = forwards(0, x0, [one])
    x1 = [crossed(ran0[i][0], 0) for i in every]
    ran1 = forwards(1, x1, ())
    kept0, kept1 = ([r[2] for r in ran] for ran in (ran0, ran1))

    back1 = backwards(1, x0, kept1)
    seed0 = [crossed(back1[i][3], 1) for i in every]
    back0 = backwards(0, seed0, kept0)
    pa = grads(0, seed0, column(kept0, 8), x0, column(kept1, 8))
    pb = grads(1, column(kept0, 6), column(back0, 0), column(kept1, 6), column(back1, 0))
    sources = [
        part
        for kept, back in ((kept0, back0), (kept1, back1))
        for part in (column(kept, 1), column(back, 2), column(kept, 4), column(back, 1))
    ]
    pc = grads(2, *sources)

    def both(a, b):
        return jnp.where(first, sum(a[1:], a[0]), sum(b[1:], b[0]))

    made = both(column(back0, 4), column(back1, 4))
    stats = both(column(ran0, 1), column(ran1, 1))[:3]
    extra = jnp.concatenate([stats, jnp.sum(counts.astype(F32)).reshape(1)])
    extra = jnp.pad(extra, (0, width - 4)).reshape(1, width)
    vec = jnp.concatenate([made[:12], extra])

    pieces = [*pa, *pb, *pc]
    if early:
        sums = []
        for p, way, start in zip(pieces, ways, starts):
            sums.append(Sum(p[0], way, flipped(p[1], start, (0, 1), size)))
        after = pc[0][0]
        for which, step in STEPS:
            if which == len(sums):
                vec, _ = lax.optimization_barrier((vec, after))
                after = vec
                vec = vec + flipped(vec, (step, step), (0, 1), size)
                if step == bits - 1:
                    after = vec
            else:
                after = sums[which].run(step, after, size)
        halves = [(s.have, s.last) for s in sums]
    else:
        halves = [lax.psum(p, "dp") for p in pieces]
        for bit in range(bits):
            vec = vec + flipped(vec, (bit, bit), (0, 1), size)

    shapes = (
        [shaped(hidden, width)],
        [shaped(width, hidden)],
        [shaped(width, 3 * width), shaped(width, width)],
    )

    def settled(half, over):
        done = []
        for k in range(3):
            mine = slice(k * PARTS, (k + 1) * PARTS)
            some = [h[half] for h in halves[mine]]
            done.append(settle(k, half * CHUNKS // 2, codes[mine], some, shapes[k], over[k]))
        return done

    (g_down,), (g_up,), (g_qkv, g_proj) = settled(1, settled(0, ((), (), ())))

    shown = jnp.stack([jnp.where(first, back0[i][3], ran1[i][0])[:slots] for i in every])
    shown = jnp.where(live, shown, jnp.zeros((), BF16))[None]
    rms = jnp.sqrt(vec[-1, 0:3] / (vec[-1, 3] * width)).reshape(1, 3)
    row = lambda k: vec[k : k + 1]
    return (
        shown,
        row(8),
        row(9),
        g_qkv[None],
        row(10),
        row(11),
        g_proj[None],
        row(0),
        row(1),
        row(2),
        g_up[None],
        vec[4 : 4 + blocks].reshape(1, hidden),
        g_down[None],
        row(3),
        rms,
    )


def solution(mesh):
    flat = P("section", None)
    deep = P("section", None, None)
    split = P("section", "dp", None, None)
    ranks = (flat, flat, deep, flat, flat, deep, flat, flat, flat, deep, flat, deep, flat)
    return jax.shard_map(
        functools.partial(per_device, mesh.shape["dp"]),
        mesh=mesh,
        in_specs=(split, P("dp"), P("section", "dp", None), *ranks),
        out_specs=(split, *ranks, flat),
        check_vma=False,
    )
```
